512 devices in a mesh: gx: 32 (over x, z_hi, core), gy: 16 (over y, z_lo).
Axes of the slice: x: 4, y: 8, z: 8 (z_hi: 4, z_lo: 2; z = z_hi * 2 + z_lo), core: 2. Of those that a mesh axis runs over, the one named last changes fastest.
Arguments:
- velocity: float32 [3, 16, 512, 2048], P(None, None, 'gx', 'gy'), may hold values from -6 to 6
- stress: float32 [6, 16, 512, 2048], P(None, None, 'gx', 'gy'), may hold values from -6 to 6
- adj_velocity: float32 [3, 16, 512, 2048], P(None, None, 'gx', 'gy'), may hold values from -6 to 6
- adj_stress: float32 [6, 16, 512, 2048], P(None, None, 'gx', 'gy'), may hold values from -6 to 6
- lame_lambda: float32 [16, 512, 2048], P(None, 'gx', 'gy'), may hold values from 0.02 to 0.06
- shear_modulus: float32 [16, 512, 2048], P(None, 'gx', 'gy'), may hold values from 0.02 to 0.06
- buoyancy: float32 [16, 512, 2048], P(None, 'gx', 'gy'), may hold values from 0.4 to 1
- gauge_cell: int32 [32, 16, 8192], P('gx', 'gy'), may hold values from 0 to 32767
- gauge_channel: int32 [32, 16, 8192], P('gx', 'gy'), may hold values from 0 to 65535, as said below
- gauge_weight: float32 [32, 16, 8192], P('gx', 'gy'), may hold values from 0.2 to 0.8
- channel_angle: float32 [16, 65536], P('gy', 'gx'), may hold values from -3.140625 to 3.140625
- observed: float32 [16, 65536], P('gy', 'gx'), may hold values from -18 to 18
Outputs:
- velocity_next: float32 [3, 16, 512, 2048], P(None, None, 'gx', 'gy')
- stress_next: float32 [6, 16, 512, 2048], P(None, None, 'gx', 'gy')
- predicted: float32 [16, 65536], P('gy', 'gx')
- adj_velocity_next: float32 [3, 16, 512, 2048], P(None, None, 'gx', 'gy')
- adj_stress_next: float32 [6, 16, 512, 2048], P(None, None, 'gx', 'gy')
The draws below stay inside these ranges and needn't reach their ends.
Inputs may be any that keep to these rules, and one draw needn't show every extreme that they name: `gauge_cell`: a local cell index z * 16 * 128 + x * 128 + y within the slot's own tile. `gauge_channel`: channel m of a row belongs to the tile at gx index m // 2048; a gauge slot of the tile at gx index i names a channel of tile i - 1, i or i + 1.
All inputs are finite; a program needn't handle non-finite values.
Results may differ from the reference program's by a relative error of at most 0.0003.
Values sent between devices are 32-bit elements; how exact they have to be, the bound alone decides.
No kernel may reach another device: no remote copies, remote signals or barrier semaphores. Data moves between devices by JAX's collectives and lax.ppermute only.
A program may use at most 64 MiB of HBM per device.

```python
import math
import jax
import jax.numpy as jnp

CX = 16
CY = 128
NZ = 16
CH_DEV = 2048
GAUGE_DEV = 8192
NX = 512
NY = 2048
CH_ROW = 65536
N_GX = 32
N_GY = 16


def draw_gauge_channel(key, part):
    side_key = jax.random.fold_in(key, 11)
    slot_key = jax.random.fold_in(key, 23)
    shape = (N_GX, N_GY, GAUGE_DEV)
    side = jax.random.randint(side_key, shape, 0, 8)
    offset = jnp.where(side == 0, -1, jnp.where(side == 7, 1, 0)).astype(jnp.int32)
    tile = jnp.clip(jnp.arange(N_GX, dtype=jnp.int32)[:, None, None] + offset, 0, N_GX - 1).astype(jnp.int32)
    within = jax.random.randint(slot_key, shape, 0, CH_DEV).astype(jnp.int32)
    return (tile * CH_DEV + within).astype(jnp.int32)


def touch_ends(result, rng, least, top_value):
    place = [jax.random.randint(jax.random.fold_in(rng, axis), (), 0, length) for axis, length in enumerate(result.shape)]
    widest = result.shape.index(max(result.shape))
    next_to = place[:widest] + [(place[widest] + 1) % result.shape[widest]] + place[widest + 1:]
    return result.at[tuple(place)].set(least).at[tuple(next_to)].set(top_value)


def block_scale(own_key, dims, shards, smallest, largest):
    def one(position, shards_of):
        draws = jax.random.uniform(jax.random.fold_in(jax.random.fold_in(own_key, 6), position), (shards_of,), jnp.float32, smallest / len(shards), largest / len(shards))
        return jnp.repeat(jnp.exp(draws), dims[position] // shards_of).reshape((-1,) + (1,) * (len(dims) - position - 1))

    level = one(*shards[0])
    for cut in shards[1:]:
        level = level * one(*cut)
    return level


def centred(key, shape, scale, reach, shards=(), held_as=jnp.bfloat16):
    array = jax.random.normal(key, shape, jnp.float32) * scale
    if len(shards) > 0:
        array = block_scale(key, shape, shards, -0.22, 0.18) * array
    return jnp.clip(array, min=-reach, max=reach).astype(held_as)


def setup_inputs(seed: int = 0) -> dict:
    key_list = jax.random.split(jax.random.key(seed), 13)
    velocity = centred(key_list[0], (3, NZ, NX, NY), 1.0, 6.0, ((2, 32), (3, 16)), jnp.float32)
    stress = centred(key_list[1], (6, NZ, NX, NY), 1.0, 6.0, ((2, 32), (3, 16)), jnp.float32)
    adj_velocity = centred(key_list[2], (3, NZ, NX, NY), 1.0, 6.0, ((2, 32), (3, 16)), jnp.float32)
    adj_stress = centred(key_list[3], (6, NZ, NX, NY), 1.0, 6.0, ((2, 32), (3, 16)), jnp.float32)
    lame_lambda = jnp.clip(jnp.exp(math.log(0.06) - 1.0986123 * jax.random.uniform(key_list[4], (NZ, NX, NY), jnp.float32) ** block_scale(key_list[4], (NZ, NX, NY), ((1, 32), (2, 16)), -0.2, 0.2)), 0.02, 0.06)
    shear_modulus = jnp.clip(jnp.exp(math.log(0.06) - 1.0986123 * jax.random.uniform(key_list[5], (NZ, NX, NY), jnp.float32) ** block_scale(key_list[5], (NZ, NX, NY), ((1, 32), (2, 16)), -0.2, 0.2)), 0.02, 0.06)
    buoyancy = jnp.clip(jnp.exp(math.log(1.0) - 0.9162907 * jax.random.uniform(key_list[6], (NZ, NX, NY), jnp.float32) ** block_scale(key_list[6], (NZ, NX, NY), ((1, 32), (2, 16)), -0.2, 0.2)), 0.4, 1.0)
    gauge_cell = touch_ends(jax.random.randint(key_list[7], (N_GX, N_GY, GAUGE_DEV), 0, NZ * CX * CY), jax.random.fold_in(key_list[7], 1), 0, (NZ * CX * CY) - 1).astype(jnp.int32)
    gauge_channel = draw_gauge_channel(jax.random.fold_in(key_list[12], 71), 0)
    gauge_weight = jnp.clip(0.2 + 0.6 * jax.random.uniform(key_list[9], (N_GX, N_GY, GAUGE_DEV), jnp.float32) ** block_scale(key_list[9], (N_GX, N_GY, GAUGE_DEV), ((0, 32), (1, 16)), -0.2, 0.2), 0.2, 0.8)
    channel_angle = jnp.clip(jax.random.uniform(key_list[10], (N_GY, CH_ROW), jnp.float32, -3.140625, 3.140625), -3.140625, 3.140625)
    observed = centred(key_list[11], (N_GY, CH_ROW), 3.0, 18.0, ((0, 16), (1, 32)), jnp.float32)
    return dict(velocity=velocity, stress=stress, adj_velocity=adj_velocity, adj_stress=adj_stress, lame_lambda=lame_lambda, shear_modulus=shear_modulus, buoyancy=buoyancy, gauge_cell=gauge_cell, gauge_channel=gauge_channel, gauge_weight=gauge_weight, channel_angle=channel_angle, observed=observed)


COEF_NEAR = 9.0 / 8.0
COEF_FAR = -1.0 / 24.0
HUBER_SQUARE = 16.0
ALONG_Z = 0
ALONG_X = 1
ALONG_Y = 2

def shifted(padded, direction, offset):
    pieces = []
    for dimension in range(3):
        extent = padded.shape[dimension] - 4
        first = 2 + (offset if dimension == direction else 0)
        pieces.append(slice(first, first + extent))
    return padded[tuple(pieces)]

def ahead(padded, direction):
    return COEF_NEAR * (shifted(padded, direction, 1) - shifted(padded, direction, 0)) + COEF_FAR * (shifted(padded, direction, 2) - shifted(padded, direction, -1))

def behind(padded, direction):
    return COEF_NEAR * (shifted(padded, direction, 0) - shifted(padded, direction, -1)) + COEF_FAR * (shifted(padded, direction, 1) - shifted(padded, direction, -2))

def velocity_change(stresses, buoyancy):
    change_x = ahead(stresses[0], ALONG_X) + behind(stresses[3], ALONG_Y) + behind(stresses[4], ALONG_Z)
    change_y = behind(stresses[3], ALONG_X) + ahead(stresses[1], ALONG_Y) + behind(stresses[5], ALONG_Z)
    change_z = behind(stresses[4], ALONG_X) + behind(stresses[5], ALONG_Y) + ahead(stresses[2], ALONG_Z)
    return buoyancy * jnp.stack([change_x, change_y, change_z])

def strain_rates(speeds):
    return (behind(speeds[0], ALONG_X), behind(speeds[1], ALONG_Y), behind(speeds[2], ALONG_Z), ahead(speeds[0], ALONG_Y) + ahead(speeds[1], ALONG_X), ahead(speeds[0], ALONG_Z) + ahead(speeds[2], ALONG_X), ahead(speeds[1], ALONG_Z) + ahead(speeds[2], ALONG_Y))

def stress_change(rates, lame_lambda, shear_modulus):
    volume = rates[0] + rates[1] + rates[2]
    return jnp.stack([lame_lambda * volume + 2.0 * shear_modulus * rates[0], lame_lambda * volume + 2.0 * shear_modulus * rates[1], lame_lambda * volume + 2.0 * shear_modulus * rates[2], shear_modulus * rates[3], shear_modulus * rates[4], shear_modulus * rates[5]])

def pad_all(fields):
    return jnp.pad(fields, ((0, 0), (2, 2), (2, 2), (2, 2)))

def reference(velocity, stress, adj_velocity, adj_stress, lame_lambda, shear_modulus, buoyancy, gauge_cell, gauge_channel, gauge_weight, channel_angle, observed):
    velocity_next = velocity + velocity_change(pad_all(stress), buoyancy)
    rates = strain_rates(pad_all(velocity_next))
    stress_next = stress + stress_change(rates, lame_lambda, shear_modulus)
    tile_x = jnp.arange(N_GX, dtype=jnp.int32)[:, None, None]
    tile_y = jnp.arange(N_GY, dtype=jnp.int32)[None, :, None]
    depth = gauge_cell // (CX * CY)
    column = tile_x * CX + gauge_cell // CY % CX
    lateral = tile_y * CY + gauge_cell % CY
    flat_cell = ((depth * NX + column) * NY + lateral).astype(jnp.int32)
    row_index = jnp.broadcast_to(tile_y, gauge_channel.shape).astype(jnp.int32)
    theta = channel_angle[row_index, gauge_channel]
    cosine = jnp.cos(theta)
    sine = jnp.sin(theta)
    rate_gauge = gauge_weight * (cosine * cosine * rates[0].reshape(-1)[flat_cell] + sine * sine * rates[1].reshape(-1)[flat_cell] + cosine * sine * rates[3].reshape(-1)[flat_cell])
    segment = (row_index * CH_ROW + gauge_channel).astype(jnp.int32)
    predicted = jax.ops.segment_sum(rate_gauge.reshape(-1), segment.reshape(-1), num_segments=N_GY * CH_ROW).reshape(N_GY, CH_ROW)
    misfit = predicted - observed
    robust = misfit / jnp.sqrt(HUBER_SQUARE + misfit * misfit)
    adj_velocity_next = adj_velocity - velocity_change(pad_all(adj_stress), buoyancy)
    adj_rates = strain_rates(pad_all(adj_velocity_next))
    pulled = adj_stress - stress_change(adj_rates, lame_lambda, shear_modulus)
    source = gauge_weight * robust[row_index, gauge_channel]
    cell_count = NZ * NX * NY
    flat_list = flat_cell.reshape(-1)

    def deposit(values):
        return jax.ops.segment_sum(values.reshape(-1), flat_list, num_segments=cell_count).reshape(NZ, NX, NY)
    empty = jnp.zeros((NZ, NX, NY), stress.dtype)
    adj_stress_next = pulled + jnp.stack([deposit(source * cosine * cosine), deposit(source * sine * sine), empty, deposit(source * cosine * sine), empty, empty])
    return (velocity_next, stress_next, predicted, adj_velocity_next, adj_stress_next)
```

```python
import functools

import jax
import jax.numpy as jnp
from jax import lax
from jax.experimental import pallas as pl
from jax.experimental.pallas import tpu as pltpu
from jax.sharding import PartitionSpec as P

C1 = 9.0 / 8.0
C2 = -1.0 / 24.0
HUBER_SQUARE = 16.0
F32 = jnp.float32
BF16 = jnp.bfloat16
VMEM_LIMIT = 40 * 1024 * 1024

N_Y = 19
EDGE = 3
Y_GROUPS = 2
UNROLL = 8


def whole():
    return pl.BlockSpec(memory_space=pltpu.VMEM)


def shape(dims, dtype=F32):
    return jax.ShapeDtypeStruct(dims, dtype)


def iota(dims, axis):
    return lax.broadcasted_iota(jnp.int32, dims, axis)


def shift_y(f, e, k):
    lane = iota(f.shape, f.ndim - 1)
    n = f.shape[-1]
    if k < 0:
        return pltpu.roll(jnp.where(lane >= n + k, e, f), -k, f.ndim - 1)
    return pltpu.roll(jnp.where(lane < k, e, f), n - k, f.ndim - 1)


def shift_x(f, h, k):
    row = iota(f.shape, f.ndim - 2)
    n = f.shape[-2]
    if k < 0:
        return pltpu.roll(jnp.where(row >= n + k, h, f), -k, f.ndim - 2)
    return pltpu.roll(jnp.where(row < k, h, f), n - k, f.ndim - 2)


def ahead(shift, f, e):
    return C1 * (shift(f, e, 1) - f) + C2 * (shift(f, e, 2) - shift(f, e, -1))


def behind(shift, f, e):
    return C1 * (f - shift(f, e, -1)) + C2 * (shift(f, e, 1) - shift(f, e, -2))


def ahead_z(ref, k, z):
    return C1 * (ref[k, z + 3] - ref[k, z + 2]) + C2 * (ref[k, z + 4] - ref[k, z + 1])


def behind_z(ref, k, z):
    return C1 * (ref[k, z + 2] - ref[k, z + 1]) + C2 * (ref[k, z + 3] - ref[k, z])


def parity(axis):
    return lax.axis_index(axis) % 2


def side(par_row, first, second):
    return jnp.where(par_row == 0, first, second)


def low_half(lane):
    return lane % (2 * EDGE) < EDGE


def pack_y_kernel(par, s, v, a_s, a_v, b, out_a, out_b, s_ref, v_ref, as_ref, av_ref, b_ref, sems):
    even = par[0] == 0
    hbm = (s, v, a_s, a_v)
    vmem = (s_ref, v_ref, as_ref, av_ref)
    depth = 16 // Y_GROUPS
    copies = []
    for g in range(Y_GROUPS):
        layers = pl.ds(g * depth, depth)
        group = [
            pltpu.make_async_copy(src.at[:, layers], dst.at[:, layers], sems.at[g, i])
            for i, (src, dst) in enumerate(zip(hbm, vmem))
        ]
        group.append(pltpu.make_async_copy(b.at[layers], b_ref.at[layers], sems.at[g, 4]))
        copies.append(group)
        for copy in group:
            copy.start()

    def packed(z):
        lane = iota((16, 128), 1)
        fields = [s_ref[k, z] for k in range(6)] + [v_ref[k, z] for k in range(3)]
        fields += [as_ref[k, z] for k in range(6)] + [av_ref[k, z] for k in range(3)] + [b_ref[z]]
        out = jnp.zeros((16, 128), F32)
        for n, f in enumerate(fields):
            out = jnp.where(lane >= 2 * EDGE * n, pltpu.roll(f, 2 * EDGE * n + EDGE, 1), out)
        return out

    def body(zz, carry):
        low = low_half(iota((16, 128), 1))
        first = packed(2 * zz)
        second = packed(2 * zz + 1)
        up = jnp.where(low, first, pltpu.roll(second, EDGE, 1))
        down = jnp.where(low, pltpu.roll(first, 128 - EDGE, 1), second)
        out_a[zz] = jnp.where(even, up, down)
        out_b[zz] = jnp.where(even, down, up)
        return carry

    for g in range(Y_GROUPS):
        for copy in copies[g]:
            copy.wait()
        lax.fori_loop(g * depth // 2, (g + 1) * depth // 2, body, 0, unroll=True)


def unpack_y_all(even_y, recv_a, recv_b, fields, e_ref, main, pads, m_ref):
    zero = jnp.zeros((16, 128), F32)
    for k in range(len(fields)):
        for z in (0, 1, 18, 19):
            e_ref[k, z] = zero
    for k in range(len(pads)):
        for z in (0, 1, 18, 19):
            m_ref[k, z] = zero

    def body(zz, carry):
        low = low_half(iota((16, 128), 1))
        ra = recv_a[zz]
        rb = recv_b[zz]
        before = jnp.where(even_y, rb, ra)
        after = jnp.where(even_y, ra, rb)
        frames = (
            jnp.where(low, before, pltpu.roll(after, EDGE, 1)),
            jnp.where(low, pltpu.roll(before, 128 - EDGE, 1), after),
        )
        for sub, frame in enumerate(frames):
            z = zz * 2 + sub
            for k, n in enumerate(fields):
                e_ref[k, z + 2] = pltpu.roll(frame, (128 - EDGE - 2 * EDGE * n) % 128, 1)
            for k, n in enumerate(pads):
                m_ref[k, z + 2] = main[n, z]
        return carry

    lax.fori_loop(0, 8, body, 0, unroll=UNROLL // 2)


def pack_x_kernel(sign, fields, n_extra, par, s, v, b, recv_a, recv_b, *rest):
    extra = rest[:n_extra]
    out_a, out_b, e_ref, m_ref = rest[n_extra:]
    even_x = par[1] == 0
    unpack_y_all(par[0] == 0, recv_a, recv_b, fields, e_ref, s, (2, 4, 5), m_ref)

    def body(z, carry):
        lane = iota((16, 128), 1)
        zero = jnp.zeros((16, 128), F32)
        sxx, syy, sxy, sxz, syz = s[0, z], s[1, z], s[3, z], s[4, z], s[5, z]
        exx, eyy, exy, exz, eyz = (e_ref[k, z + 2] for k in (0, 1, 3, 4, 5))
        by = b[z]
        cx = ahead(shift_x, sxx, zero) + behind(shift_y, sxy, exy) + behind_z(m_ref, 1, z)
        cy = behind(shift_x, sxy, zero) + ahead(shift_y, syy, eyy) + behind_z(m_ref, 2, z)
        cz = behind(shift_x, sxz, zero) + behind(shift_y, syz, eyz) + ahead_z(m_ref, 0, z)
        ep = jnp.where(lane < 3, exx, zero)
        ep = jnp.where(lane >= 125, exx, ep)
        ep = jnp.where((lane >= 5) & (lane < 11), pltpu.roll(exy, 8, 1), ep)
        ep = jnp.where((lane >= 13) & (lane < 19), pltpu.roll(exz, 16, 1), ep)
        items = [v[0, z] + sign * (by * cx), v[1, z] + sign * (by * cy), v[2, z] + sign * (by * cz)]
        items += [by, sxx, sxy, sxz, ep]
        up = jnp.concatenate([f[14:16] for f in items], axis=0)
        down = jnp.concatenate([f[0:2] for f in items], axis=0)
        out_a[z] = jnp.where(even_x, up, down)
        out_b[z] = jnp.where(even_x, down, up)
        return carry

    lax.fori_loop(0, 16, body, 0, unroll=UNROLL)
    for k in range(n_extra // 2):
        out_a[16 + k] = extra[2 * k][...]
        out_b[16 + k] = extra[2 * k + 1][...]


def spread_rows(before, after, k):
    row = iota((16, 128), 0)
    left = pltpu.roll(before, (14 - 2 * k) % 16, 0) if k != 7 else before
    right = pltpu.roll(after, (16 - 2 * k) % 16, 0) if k else after
    return jnp.where(row < 8, right, left)


def step_kernel(
    sign, fields, with_rates, own_b, par, s, v, b, lam, mu, recv_ya, recv_yb, recv_xa, recv_xb, *rest
):
    if own_b:
        v_out, s_out = rest[:2]
        rest = rest[2:]
    else:
        bxa, bxb, v_out, s_out = rest[:4]
        rest = rest[4:]
    if with_rates:
        r_out = rest[0]
        rest = rest[1:]
    e_ref, m_ref, vm_ref, ve_ref, vh_ref = rest
    even_x = par[1] == 0
    unpack_y_all(par[0] == 0, recv_ya, recv_yb, fields, e_ref, s, (2, 4, 5), m_ref)
    zero = jnp.zeros((16, 128), F32)
    for k in range(3):
        for z in (0, 1, 18, 19):
            vm_ref[k, z] = zero

    def speeds(z, carry):
        xa = recv_xa[z]
        xb = recv_xb[z]
        before = jnp.where(even_x, xb, xa)
        after = jnp.where(even_x, xa, xb)
        hx, hy, hz, hb, hxx, hxy, hxz, hp = (spread_rows(before, after, k) for k in range(8))
        if not own_b:
            ba = bxa[z]
            bb = bxb[z]
            hb = spread_rows(jnp.where(even_x, bb, ba), jnp.where(even_x, ba, bb), 3)
        hpy = pltpu.roll(hp, 120, 1)
        hpz = pltpu.roll(hp, 112, 1)
        sxx, syy, sxy, sxz, syz = s[0, z], s[1, z], s[3, z], s[4, z], s[5, z]
        exx, eyy, exy, exz, eyz = (e_ref[k, z + 2] for k in (0, 1, 3, 4, 5))
        by = b[z]
        be = e_ref[9, z + 2]
        cx = ahead(shift_x, sxx, hxx) + behind(shift_y, sxy, exy) + behind_z(m_ref, 1, z)
        cy = behind(shift_x, sxy, hxy) + ahead(shift_y, syy, eyy) + behind_z(m_ref, 2, z)
        cz = behind(shift_x, sxz, hxz) + behind(shift_y, syz, eyz) + ahead_z(m_ref, 0, z)
        for k, c in enumerate((cx, cy, cz)):
            new = v[k, z] + sign * (by * c)
            vm_ref[k, z + 2] = new
            v_out[k, z] = new
        cx = ahead(shift_x, exx, hp) + behind(shift_y, exy, sxy) + behind_z(e_ref, 4, z)
        cy = behind(shift_x, exy, hpy) + ahead(shift_y, eyy, syy) + behind_z(e_ref, 5, z)
        cz = behind(shift_x, exz, hpz) + behind(shift_y, eyz, syz) + ahead_z(e_ref, 2, z)
        for k, c in enumerate((cx, cy, cz)):
            ve_ref[k, z] = e_ref[6 + k, z + 2] + sign * (be * c)
        vh_ref[0, z] = hx + sign * (hb * ahead(shift_x, zero, sxx))
        vh_ref[1, z] = hy + sign * (hb * behind(shift_x, zero, sxy))
        vh_ref[2, z] = hz + sign * (hb * behind(shift_x, zero, sxz))
        return carry

    lax.fori_loop(0, 16, speeds, 0, unroll=UNROLL)

    def rates(z, carry):
        vx, vy, vz = (vm_ref[k, z + 2] for k in range(3))
        ex, ey, ez = (ve_ref[k, z] for k in range(3))
        hx, hy, hz = (vh_ref[k, z] for k in range(3))
        r0 = behind(shift_x, vx, hx)
        r1 = behind(shift_y, vy, ey)
        r2 = behind_z(vm_ref, 2, z)
        r3 = ahead(shift_y, vx, ex) + ahead(shift_x, vy, hy)
        r4 = ahead_z(vm_ref, 0, z) + ahead(shift_x, vz, hz)
        r5 = ahead_z(vm_ref, 1, z) + ahead(shift_y, vz, ez)
        m = mu[z]
        volume = lam[z] * (r0 + r1 + r2)
        m2 = 2.0 * m
        for k, c in enumerate((volume + m2 * r0, volume + m2 * r1, volume + m2 * r2, m * r3, m * r4, m * r5)):
            s_out[k, z] = s[k, z] + sign * c
        if with_rates:
            r_out[0, z] = r0
            r_out[1, z] = r1
            r_out[2, z] = r3
        return carry

    lax.fori_loop(0, 16, rates, 0, unroll=UNROLL)


CHUNK = 4096
TILE = CHUNK // 128
ROWS = 64


def pieces(x, n):
    out = []
    for _ in range(n):
        p = x.astype(BF16)
        out.append(p)
        x = x - p.astype(F32)
    return out


def lanes_of(ref, q):
    return jnp.concatenate([ref[pl.ds(q * TILE + i, 1), :] for i in range(TILE)], axis=1)


def put_lanes(ref, k, q, row):
    for i in range(TILE):
        ref[k, pl.ds(q * TILE + i, 1), :] = row[:, 128 * i : 128 * (i + 1)]


def one_hot(index, n):
    return (iota((n, index.shape[1]), 0) == index).astype(F32).astype(BF16)


def pick(out, low, n):
    acc = jnp.zeros((8, out.shape[1]), F32)
    for t in range(n // 8):
        hit = iota(acc.shape, 0) + 8 * t == low
        acc = acc + jnp.where(hit, out[8 * t : 8 * t + 8], 0.0)
    return jnp.sum(acc, axis=0, keepdims=True)


def dot(a, b):
    return jnp.dot(a, b, preferred_element_type=F32)


def dot_nt(a, b):
    return lax.dot_general(a, b, (((1,), (1,)), ((), ())), preferred_element_type=F32)


def pick_channel(q, table, chan):
    c = lanes_of(chan, q)
    high = one_hot(c >> 7, 48)
    out = dot(table, jnp.concatenate([high] * 3, axis=0))
    return pick(out, c & 127, 128)


def channel_table(rows):
    return jnp.concatenate(pieces(rows.T, 3), axis=1)


def sample_kernel(par, cell, chan_raw, weight, angle_a, angle, angle_b, rates, part, trig, chan, table, rows, vals):
    chan[...] = chan_raw[...] - par[2]
    even_x = par[1] == 0
    aa = angle_a[...]
    ab = angle_b[...]
    angles = jnp.concatenate([jnp.where(even_x, ab, aa), angle[...], jnp.where(even_x, aa, ab)], axis=0)
    ang = channel_table(angles)
    for k in range(3):
        hi, lo = pieces(rates[k].T, 2)
        table[128 * k : 128 * (k + 1)] = hi
        table[384 + 128 * k : 384 + 128 * (k + 1)] = lo

    def gather(q, carry):
        put_lanes(rows, 0, q, pick_channel(q, ang, chan))
        c = lanes_of(cell, q)
        out = dot(table[...], one_hot(c >> 7, 256))
        low = c & 127
        for k in range(3):
            both = out[128 * k : 128 * (k + 1)] + out[384 + 128 * k : 384 + 128 * (k + 1)]
            put_lanes(rows, 1 + k, q, pick(both, low, 128))
        return carry

    lax.fori_loop(0, 8192 // CHUNK, gather, 0)
    theta = rows[0]
    cosine = jnp.cos(theta)
    sine = jnp.sin(theta)
    w = weight[...]
    t0 = w * (cosine * cosine)
    t1 = w * (sine * sine)
    t2 = w * (cosine * sine)
    trig[0] = t0
    trig[1] = t1
    trig[2] = t2
    value = t0 * rows[1] + t1 * rows[2] + t2 * rows[3]
    for k, p in enumerate(pieces(value, 3)):
        vals[k] = p.astype(F32)

    def scatter(q, acc):
        c = lanes_of(chan, q)
        hit = iota((48, CHUNK), 0) == c >> 7
        a = jnp.concatenate([jnp.where(hit, lanes_of(vals.at[k], q), 0.0) for k in range(3)], axis=0)
        return acc + dot_nt(a.astype(BF16), one_hot(c & 127, 128))

    acc = lax.fori_loop(0, 8192 // CHUNK, scatter, jnp.zeros((144, 128), F32))
    part[...] = acc[0:48] + acc[48:96] + acc[96:144]


def deposit_kernel(par, cell, chan_raw, trig, robust_a, robust, robust_b, pulled, out, chan, vals, acc):
    chan[...] = chan_raw[...] - par[2]
    even_x = par[1] == 0
    ra = robust_a[...]
    rb = robust_b[...]
    tab = channel_table(
        jnp.concatenate([jnp.where(even_x, rb, ra), robust[...], jnp.where(even_x, ra, rb)], axis=0)
    )

    def gather(q, carry):
        put_lanes(vals, 6, q, pick_channel(q, tab, chan))
        return carry

    lax.fori_loop(0, 8192 // CHUNK, gather, 0)
    rob = vals[6]
    for k in range(3):
        for i, p in enumerate(pieces(trig[k] * rob, 2)):
            vals[2 * k + i] = p.astype(F32)
    acc[...] = jnp.zeros(acc.shape, F32)

    def place(q, carry):
        c = lanes_of(cell, q)
        hit = iota((128, CHUNK), 0) == c & 127
        b = jnp.concatenate([jnp.where(hit, lanes_of(vals.at[k], q), 0.0).astype(BF16) for k in range(6)], axis=0)
        acc[...] += dot_nt(one_hot(c >> 7, 256), b)
        return carry

    lax.fori_loop(0, 8192 // CHUNK, place, 0)
    for k in (2, 4, 5):
        out[k] = pulled[k]
    for n, k in enumerate((0, 1, 3)):
        out[k] = pulled[k] + acc[:, 256 * n : 256 * n + 128] + acc[:, 256 * n + 128 : 256 * n + 256]


def pairs(axis, first):
    size = lax.axis_size(axis)
    route = []
    for i in range(first, size - 1, 2):
        route += [(i, i + 1), (i + 1, i)]
    return route


def swap(a, b, axis):
    return (lax.ppermute(a, axis, pairs(axis, 0)), lax.ppermute(b, axis, pairs(axis, 1)))


def call(kernel, outs, n_in, scratch, name, space=pltpu.VMEM):
    return pl.pallas_call(
        kernel,
        out_shape=outs,
        in_specs=[pl.BlockSpec(memory_space=pltpu.SMEM)] + [pl.BlockSpec(memory_space=space)] * n_in,
        out_specs=jax.tree.map(lambda _: whole(), outs),
        scratch_shapes=scratch,
        compiler_params=pltpu.CompilerParams(vmem_limit_bytes=VMEM_LIMIT),
        name=name,
    )


def shards(
    velocity,
    stress,
    adj_velocity,
    adj_stress,
    lame_lambda,
    shear_modulus,
    buoyancy,
    gauge_cell,
    gauge_channel,
    gauge_weight,
    channel_angle,
    observed,
):
    owned = observed.shape[1]
    gx = lax.axis_index("gx")
    gy = lax.axis_index("gy")
    par = jnp.stack([gy % 2, gx % 2, (gx - 1) * owned]).astype(jnp.int32)
    even_x = gx % 2 == 0
    slots = (ROWS, 128)
    cell = gauge_cell.reshape(slots)
    chan = gauge_channel.reshape(slots)
    weight = gauge_weight.reshape(slots)
    angle = channel_angle.reshape(16, 128)

    slab = shape((8, 16, 128))
    msg_a, msg_b = call(
        pack_y_kernel,
        (slab, slab),
        5,
        [pltpu.VMEM(f.shape, F32) for f in (stress, velocity, adj_stress, adj_velocity, buoyancy)]
        + [pltpu.SemaphoreType.DMA((Y_GROUPS, 5))],
        "pack_y",
        pltpu.HBM,
    )(
        par, stress, velocity, adj_stress, adj_velocity, buoyancy
    )
    ya, yb = swap(msg_a, msg_b, "gy")

    e_scratch = pltpu.VMEM((10, 20, 16, 128), F32)
    m_scratch = pltpu.VMEM((3, 20, 16, 128), F32)
    fields_f = tuple(range(9)) + (18,)
    fields_a = tuple(range(9, 18)) + (18,)
    msg = shape((17, 16, 128))
    fa, fb = call(
        functools.partial(pack_x_kernel, 1.0, fields_f, 2), (msg, msg), 7, [e_scratch, m_scratch], "pack_x"
    )(par, stress, velocity, buoyancy, ya, yb, angle, angle)
    fa, fb = swap(fa, fb, "gx")
    msg = shape((16, 16, 128))
    aa, ab = call(
        functools.partial(pack_x_kernel, -1.0, fields_a, 0), (msg, msg), 5, [e_scratch, m_scratch], "pack_x_adj"
    )(par, adj_stress, adj_velocity, buoyancy, ya, yb)

    speed = shape((3, 16, 16, 128))
    tensor = shape((6, 16, 16, 128))
    v_scratch = [pltpu.VMEM((3, 20, 16, 128), F32)] + [pltpu.VMEM((3, 16, 16, 128), F32)] * 2
    velocity_next, stress_next, rates = call(
        functools.partial(step_kernel, 1.0, fields_f, True, True),
        (speed, tensor, speed),
        9,
        [e_scratch, m_scratch] + v_scratch,
        "step",
    )(par, stress, velocity, buoyancy, lame_lambda, shear_modulus, ya, yb, fa, fb)

    part, trig = call(
        sample_kernel,
        (shape((48, 128)), shape((3,) + slots)),
        7,
        [
            pltpu.VMEM(slots, jnp.int32),
            pltpu.VMEM((768, 256), BF16),
            pltpu.VMEM((4,) + slots, F32),
            pltpu.VMEM((3,) + slots, F32),
        ],
        "sample",
    )(par, cell, chan, weight, fa[16], angle, fb[16], rates.reshape(3, 256, 128))

    to_after = part[32:48]
    to_before = part[0:16]
    send_a = jnp.concatenate([aa, jnp.where(even_x, to_after, to_before)[None]], axis=0)
    send_b = jnp.concatenate([ab, jnp.where(even_x, to_before, to_after)[None]], axis=0)
    aa, ab = swap(send_a, send_b, "gx")
    predicted = part[16:32] + aa[16] + ab[16]
    misfit = predicted - observed.reshape(16, 128)
    robust = misfit / jnp.sqrt(HUBER_SQUARE + misfit * misfit)
    robust_a, robust_b = swap(robust, robust, "gx")

    adj_velocity_next, pulled = call(
        functools.partial(step_kernel, -1.0, fields_a, False, False),
        (speed, tensor),
        11,
        [e_scratch, m_scratch] + v_scratch,
        "step_adj",
    )(par, adj_stress, adj_velocity, buoyancy, lame_lambda, shear_modulus, ya, yb, aa, ab, fa, fb)

    adj_stress_next = call(
        deposit_kernel,
        shape((6, 256, 128)),
        7,
        [
            pltpu.VMEM(slots, jnp.int32),
            pltpu.VMEM((7,) + slots, F32),
            pltpu.VMEM((256, 768), F32),
        ],
        "deposit",
    )(par, cell, chan, trig, robust_a, robust, robust_b, pulled.reshape(6, 256, 128)).reshape(tensor.shape)
    return (velocity_next, stress_next, predicted.reshape(1, owned), adj_velocity_next, adj_stress_next)


def solution(mesh):
    field = P(None, None, "gx", "gy")
    scalar = P(None, "gx", "gy")
    slot = P("gx", "gy", None)
    row = P("gy", "gx")
    return jax.shard_map(
        shards,
        mesh=mesh,
        in_specs=(field,) * 4 + (scalar,) * 3 + (slot,) * 3 + (row,) * 2,
        out_specs=(field, field, row, field, field),
        check_vma=False,
    )
```

```python
import functools

import jax
import jax.numpy as jnp
from jax import lax
from jax.experimental import pallas as pl
from jax.experimental.pallas import tpu as pltpu
from jax.sharding import PartitionSpec as P

C1 = 9.0 / 8.0
C2 = -1.0 / 24.0
HUBER_SQUARE = 16.0
F32 = jnp.float32
BF16 = jnp.bfloat16
VMEM_LIMIT = 40 * 1024 * 1024

N_Y = 19
EDGE = 3
Y_GROUPS = 2
UNROLL = 8


def whole():
    return pl.BlockSpec(memory_space=pltpu.VMEM)


def shape(dims, dtype=F32):
    return jax.ShapeDtypeStruct(dims, dtype)


def iota(dims, axis):
    return lax.broadcasted_iota(jnp.int32, dims, axis)


def shift_y(f, e, k):
    lane = iota(f.shape, f.ndim - 1)
    n = f.shape[-1]
    if k < 0:
        return pltpu.roll(jnp.where(lane >= n + k, e, f), -k, f.ndim - 1)
    return pltpu.roll(jnp.where(lane < k, e, f), n - k, f.ndim - 1)


def shift_x(f, h, k):
    row = iota(f.shape, f.ndim - 2)
    n = f.shape[-2]
    if k < 0:
        return pltpu.roll(jnp.where(row >= n + k, h, f), -k, f.ndim - 2)
    return pltpu.roll(jnp.where(row < k, h, f), n - k, f.ndim - 2)


def ahead(shift, f, e):
    return C1 * (shift(f, e, 1) - f) + C2 * (shift(f, e, 2) - shift(f, e, -1))


def behind(shift, f, e):
    return C1 * (f - shift(f, e, -1)) + C2 * (shift(f, e, 1) - shift(f, e, -2))


def ahead_z(ref, k, z):
    return C1 * (ref[k, z + 3] - ref[k, z + 2]) + C2 * (ref[k, z + 4] - ref[k, z + 1])


def behind_z(ref, k, z):
    return C1 * (ref[k, z + 2] - ref[k, z + 1]) + C2 * (ref[k, z + 3] - ref[k, z])


def parity(axis):
    return lax.axis_index(axis) % 2


def side(par_row, first, second):
    return jnp.where(par_row == 0, first, second)


def low_half(lane):
    return lane % (2 * EDGE) < EDGE


def pack_y_kernel(par, s, v, a_s, a_v, b, out_a, out_b, s_ref, v_ref, as_ref, av_ref, b_ref, sems):
    even = par[0] == 0
    hbm = (s, v, a_s, a_v)
    vmem = (s_ref, v_ref, as_ref, av_ref)
    depth = 16 // Y_GROUPS
    copies = []
    for g in range(Y_GROUPS):
        layers = pl.ds(g * depth, depth)
        group = [
            pltpu.make_async_copy(src.at[:, layers], dst.at[:, layers], sems.at[g, i])
            for i, (src, dst) in enumerate(zip(hbm, vmem))
        ]
        group.append(pltpu.make_async_copy(b.at[layers], b_ref.at[layers], sems.at[g, 4]))
        copies.append(group)
        for copy in group:
            copy.start()

    def packed(z):
        lane = iota((16, 128), 1)
        fields = [s_ref[k, z] for k in range(6)] + [v_ref[k, z] for k in range(3)]
        fields += [as_ref[k, z] for k in range(6)] + [av_ref[k, z] for k in range(3)] + [b_ref[z]]
        out = jnp.zeros((16, 128), F32)
        for n, f in enumerate(fields):
            out = jnp.where(lane >= 2 * EDGE * n, pltpu.roll(f, 2 * EDGE * n + EDGE, 1), out)
        return out

    def body(zz, carry):
        low = low_half(iota((16, 128), 1))
        first = packed(2 * zz)
        second = packed(2 * zz + 1)
        up = jnp.where(low, first, pltpu.roll(second, EDGE, 1))
        down = jnp.where(low, pltpu.roll(first, 128 - EDGE, 1), second)
        out_a[zz] = jnp.where(even, up, down)
        out_b[zz] = jnp.where(even, down, up)
        return carry

    for g in range(Y_GROUPS):
        for copy in copies[g]:
            copy.wait()
        lax.fori_loop(g * depth // 2, (g + 1) * depth // 2, body, 0, unroll=True)


UP = (0, 7, 4, 5, 6, 8, 12, 13, 14, 1, 2, 3, 9, 10, 11)
DOWN = (1, 2, 7, 3, 6, 9, 10, 11, 14, 0, 4, 5, 8, 12, 13)
PAIRED = 9
MSG_ROWS = 24


def slot(order, item):
    at = order.index(item)
    return 2 * at if at < PAIRED else PAIRED + at


def put_rows(acc, order, item, block, first):
    at = slot(order, item)
    width = 2 if order.index(item) < PAIRED else 1
    src = first if width == 2 or first == 0 else first + 1
    row = iota((8, 128), 0)
    lo = at % 8
    moved = pltpu.roll(block, (lo - src) % 8, 0) if (lo - src) % 8 else block
    acc[at // 8] = jnp.where((row >= lo) & (row < lo + width), moved, acc[at // 8])


def get_rows(msg, order, item, first):
    at = slot(order, item)
    width = 2 if order.index(item) < PAIRED else 1
    src = first if width == 2 or first == 0 else first + 1
    block = msg[8 * (at // 8) : 8 * (at // 8) + 8]
    turn = (src - at % 8) % 8
    return pltpu.roll(block, turn, 0) if turn else block


def pack_x_kernel(par, s, v, a_s, a_v, b, angle, recv_a, recv_b, out_a, out_b, pv, a_pv, e, a_e, m, a_m):
    even_y = par[0] == 0
    even_x = par[1] == 0
    zero = jnp.zeros((16, 128), F32)
    for ref, n in ((e, 10), (a_e, 9), (m, 3), (a_m, 3)):
        for k in range(n):
            for z in (0, 1, 18, 19):
                ref[k, z] = zero

    def frames(zz, carry):
        low = low_half(iota((16, 128), 1))
        ra = recv_a[zz]
        rb = recv_b[zz]
        before = jnp.where(even_y, rb, ra)
        after = jnp.where(even_y, ra, rb)
        both = (
            jnp.where(low, before, pltpu.roll(after, EDGE, 1)),
            jnp.where(low, pltpu.roll(before, 128 - EDGE, 1), after),
        )
        for sub, frame in enumerate(both):
            z = zz * 2 + sub
            for n in range(N_Y):
                value = pltpu.roll(frame, (128 - EDGE - 2 * EDGE * n) % 128, 1)
                if n < 9:
                    e[n, z + 2] = value
                elif n < 18:
                    a_e[n - 9, z + 2] = value
                else:
                    e[9, z + 2] = value
            for k, n in enumerate((2, 4, 5)):
                m[k, z + 2] = s[n, z]
                a_m[k, z + 2] = a_s[n, z]
        return carry

    lax.fori_loop(0, 8, frames, 0, unroll=UNROLL // 2)

    def body(z, carry):
        lane = iota((16, 128), 1)
        by = b[z]
        up = [jnp.zeros((8, 128), F32)] * 3
        down = [jnp.zeros((8, 128), F32)] * 3
        for base, sign, s_ref, v_ref, e_ref, m_ref, out in (
            (0, 1.0, s, v, e, m, pv),
            (8, -1.0, a_s, a_v, a_e, a_m, a_pv),
        ):
            sxx, syy, sxy, sxz, syz = (s_ref[k, z] for k in (0, 1, 3, 4, 5))
            exx, eyy, exy, exz, eyz = (e_ref[k, z + 2] for k in (0, 1, 3, 4, 5))
            cx = ahead(shift_x, sxx, zero) + behind(shift_y, sxy, exy) + behind_z(m_ref, 1, z)
            cy = behind(shift_x, sxy, zero) + ahead(shift_y, syy, eyy) + behind_z(m_ref, 2, z)
            cz = behind(shift_x, sxz, zero) + behind(shift_y, syz, eyz) + ahead_z(m_ref, 0, z)
            ep = jnp.where((lane >= 5) & (lane < 11), pltpu.roll(exy, 8, 1), exx)
            ep = jnp.where((lane >= 13) & (lane < 19), pltpu.roll(exz, 16, 1), ep)
            speeds = [v_ref[k, z] + sign * (by * c) for k, c in enumerate((cx, cy, cz))]
            for k in range(3):
                out[k, z] = speeds[k]
            items = speeds + [sxx, sxy, sxz, ep] + ([by] if base == 0 else [])
            for k, f in enumerate(items):
                put_rows(up, UP, base + k, f[8:16], 6)
                put_rows(down, DOWN, base + k, f[0:8], 0)
        for t in range(3):
            rows = slice(8 * t, 8 * t + 8)
            out_a[z, rows] = jnp.where(even_x, up[t], down[t])
            out_b[z, rows] = jnp.where(even_x, down[t], up[t])
        return carry

    lax.fori_loop(0, 16, body, 0, unroll=UNROLL)
    for ref in (out_a, out_b):
        ref[16, 0:16] = angle[...]
        ref[16, 16:24] = jnp.zeros((8, 128), F32)


def frame_kernel(s, a_s, e, a_e, out, a_out):
    zero = jnp.zeros((16, 128), F32)

    def body(z, carry):
        be = e[9, z + 2]
        for sign, s_ref, e_ref, o in ((1.0, s, e, out), (-1.0, a_s, a_e, a_out)):
            syy, sxy, syz = (s_ref[k, z] for k in (1, 3, 5))
            exx, eyy, exy, exz, eyz = (e_ref[k, z + 2] for k in (0, 1, 3, 4, 5))
            cx = ahead(shift_x, exx, zero) + behind(shift_y, exy, sxy) + behind_z(e_ref, 4, z)
            cy = behind(shift_x, exy, zero) + ahead(shift_y, eyy, syy) + behind_z(e_ref, 5, z)
            cz = behind(shift_x, exz, zero) + behind(shift_y, eyz, syz) + ahead_z(e_ref, 2, z)
            for k, c in enumerate((cx, cy, cz)):
                o[k, z] = e_ref[6 + k, z + 2] + sign * (be * c)
        return carry

    lax.fori_loop(0, 16, body, 0, unroll=UNROLL)


def masked_roll(block, k, low, high):
    row = iota((8, 128), 0)
    return jnp.where((row >= low) & (row < high), pltpu.roll(block, k % 8, 0), 0.0)


def ahead_first(block):
    return -C2 * masked_roll(block, 1, 0, 1)


def ahead_last(block):
    return C1 * masked_roll(block, -1, 7, 8) + C2 * masked_roll(block, -2, 6, 8)


def behind_first(block):
    return -C1 * masked_roll(block, 1, 0, 1) - C2 * masked_roll(block, 2, 0, 2)


def behind_last(block):
    return C2 * masked_roll(block, -1, 7, 8)


ADDED = ((ahead_first, ahead_last), (behind_first, behind_last), (behind_first, behind_last))


def step_kernel(sign, base, par, s, pv, pve, b, be, lam, mu, recv_a, recv_b, v_out, s_out, *rest):
    r_out = rest[0] if len(rest) == 4 else None
    vm_ref, ve_ref, vh_ref = rest[-3:]
    even_x = par[1] == 0
    zero = jnp.zeros((16, 128), F32)
    for k in range(3):
        for z in (0, 1, 18, 19):
            vm_ref[k, z] = zero

    def speeds(z, carry):
        xa = recv_a[z]
        xb = recv_b[z]
        before = jnp.where(even_x, xb, xa)
        after = jnp.where(even_x, xa, xb)

        def halo(item):
            return (get_rows(before, UP, item, 6), get_rows(after, DOWN, item, 0))

        b_left, b_right = halo(7)
        p_left, p_right = halo(base + 6)
        by = b[z]
        bf = be[0, z + 2]
        for k, (first, last) in enumerate(ADDED):
            left, right = halo(base + 3 + k)
            new = pv[k, z] + sign * (by * jnp.concatenate([first(left), last(right)], axis=0))
            vm_ref[k, z + 2] = new
            v_out[k, z] = new
            turn = (128 - 8 * k) % 128
            e_left = pltpu.roll(p_left, turn, 1) if turn else p_left
            e_right = pltpu.roll(p_right, turn, 1) if turn else p_right
            ve_ref[k, z] = pve[k, z] + sign * (bf * jnp.concatenate([first(e_left), last(e_right)], axis=0))
            v_left, v_right = halo(base + k)
            f = s[(0, 3, 4)[k], z]
            vh_ref[k, z, 0:8] = v_right + sign * (b_right * first(f[8:16]))
            vh_ref[k, z, 8:16] = v_left + sign * (b_left * last(f[0:8]))
        return carry

    lax.fori_loop(0, 16, speeds, 0, unroll=UNROLL)

    def rates(z, carry):
        vx, vy, vz = (vm_ref[k, z + 2] for k in range(3))
        ex, ey, ez = (ve_ref[k, z] for k in range(3))
        hx, hy, hz = (vh_ref[k, z] for k in range(3))
        r0 = behind(shift_x, vx, hx)
        r1 = behind(shift_y, vy, ey)
        r2 = behind_z(vm_ref, 2, z)
        r3 = ahead(shift_y, vx, ex) + ahead(shift_x, vy, hy)
        r4 = ahead_z(vm_ref, 0, z) + ahead(shift_x, vz, hz)
        r5 = ahead_z(vm_ref, 1, z) + ahead(shift_y, vz, ez)
        m = mu[z]
        volume = lam[z] * (r0 + r1 + r2)
        m2 = 2.0 * m
        for k, c in enumerate((volume + m2 * r0, volume + m2 * r1, volume + m2 * r2, m * r3, m * r4, m * r5)):
            s_out[k, z] = s[k, z] + sign * c
        if r_out is not None:
            r_out[0, z] = r0
            r_out[1, z] = r1
            r_out[2, z] = r3
        return carry

    lax.fori_loop(0, 16, rates, 0, unroll=UNROLL)


CHUNK = 4096
TILE = CHUNK // 128
ROWS = 64


def pieces(x, n):
    out = []
    for _ in range(n):
        p = x.astype(BF16)
        out.append(p)
        x = x - p.astype(F32)
    return out


def lanes_of(ref, q):
    return jnp.concatenate([ref[pl.ds(q * TILE + i, 1), :] for i in range(TILE)], axis=1)


def put_lanes(ref, k, q, row):
    for i in range(TILE):
        ref[k, pl.ds(q * TILE + i, 1), :] = row[:, 128 * i : 128 * (i + 1)]


def one_hot(index, n):
    return (iota((n, index.shape[1]), 0) == index).astype(F32).astype(BF16)


def pick(out, low, n):
    acc = jnp.zeros((8, out.shape[1]), F32)
    for t in range(n // 8):
        hit = iota(acc.shape, 0) + 8 * t == low
        acc = acc + jnp.where(hit, out[8 * t : 8 * t + 8], 0.0)
    return jnp.sum(acc, axis=0, keepdims=True)


def dot(a, b):
    return jnp.dot(a, b, preferred_element_type=F32)


def dot_nt(a, b):
    return lax.dot_general(a, b, (((1,), (1,)), ((), ())), preferred_element_type=F32)


def pick_channel(q, table, chan):
    c = lanes_of(chan, q)
    high = one_hot(c >> 7, 48)
    out = dot(table, jnp.concatenate([high] * 3, axis=0))
    return pick(out, c & 127, 128)


def channel_table(rows):
    return jnp.concatenate(pieces(rows.T, 3), axis=1)


def sample_kernel(
    par, cell, chan_raw, weight, recv_a, angle, recv_b, rates, part, part_a, part_b, trig, chan, table, rows, vals
):
    chan[...] = chan_raw[...] - par[2]
    even_x = par[1] == 0
    aa = recv_a[16, 0:16]
    ab = recv_b[16, 0:16]
    angles = jnp.concatenate([jnp.where(even_x, ab, aa), angle[...], jnp.where(even_x, aa, ab)], axis=0)
    ang = channel_table(angles)
    for k in range(3):
        hi, lo = pieces(rates[k].T, 2)
        table[128 * k : 128 * (k + 1)] = hi
        table[384 + 128 * k : 384 + 128 * (k + 1)] = lo

    def gather(q, carry):
        put_lanes(rows, 0, q, pick_channel(q, ang, chan))
        c = lanes_of(cell, q)
        out = dot(table[...], one_hot(c >> 7, 256))
        low = c & 127
        for k in range(3):
            both = out[128 * k : 128 * (k + 1)] + out[384 + 128 * k : 384 + 128 * (k + 1)]
            put_lanes(rows, 1 + k, q, pick(both, low, 128))
        return carry

    lax.fori_loop(0, 8192 // CHUNK, gather, 0)
    theta = rows[0]
    cosine = jnp.cos(theta)
    sine = jnp.sin(theta)
    w = weight[...]
    t0 = w * (cosine * cosine)
    t1 = w * (sine * sine)
    t2 = w * (cosine * sine)
    trig[0] = t0
    trig[1] = t1
    trig[2] = t2
    value = t0 * rows[1] + t1 * rows[2] + t2 * rows[3]
    for k, p in enumerate(pieces(value, 3)):
        vals[k] = p.astype(F32)

    def scatter(q, acc):
        c = lanes_of(chan, q)
        hit = iota((48, CHUNK), 0) == c >> 7
        a = jnp.concatenate([jnp.where(hit, lanes_of(vals.at[k], q), 0.0) for k in range(3)], axis=0)
        return acc + dot_nt(a.astype(BF16), one_hot(c & 127, 128))

    acc = lax.fori_loop(0, 8192 // CHUNK, scatter, jnp.zeros((144, 128), F32))
    total = acc[0:48] + acc[48:96] + acc[96:144]
    part[...] = total[16:32]
    part_a[...] = jnp.where(even_x, total[32:48], total[0:16])
    part_b[...] = jnp.where(even_x, total[0:16], total[32:48])


def deposit_kernel(par, cell, chan_raw, trig, robust_a, robust, robust_b, pulled, out, chan, vals, acc):
    chan[...] = chan_raw[...] - par[2]
    even_x = par[1] == 0
    ra = robust_a[...]
    rb = robust_b[...]
    tab = channel_table(
        jnp.concatenate([jnp.where(even_x, rb, ra), robust[...], jnp.where(even_x, ra, rb)], axis=0)
    )

    def gather(q, carry):
        put_lanes(vals, 6, q, pick_channel(q, tab, chan))
        return carry

    lax.fori_loop(0, 8192 // CHUNK, gather, 0)
    rob = vals[6]
    for k in range(3):
        for i, p in enumerate(pieces(trig[k] * rob, 2)):
            vals[2 * k + i] = p.astype(F32)
    acc[...] = jnp.zeros(acc.shape, F32)

    def place(q, carry):
        c = lanes_of(cell, q)
        hit = iota((128, CHUNK), 0) == c & 127
        b = jnp.concatenate([jnp.where(hit, lanes_of(vals.at[k], q), 0.0).astype(BF16) for k in range(6)], axis=0)
        acc[...] += dot_nt(one_hot(c >> 7, 256), b)
        return carry

    lax.fori_loop(0, 8192 // CHUNK, place, 0)
    for k in (2, 4, 5):
        out[k] = pulled[k]
    for n, k in enumerate((0, 1, 3)):
        out[k] = pulled[k] + acc[:, 256 * n : 256 * n + 128] + acc[:, 256 * n + 128 : 256 * n + 256]


def pairs(axis, first):
    size = lax.axis_size(axis)
    route = []
    for i in range(first, size - 1, 2):
        route += [(i, i + 1), (i + 1, i)]
    return route


def swap(a, b, axis):
    return (lax.ppermute(a, axis, pairs(axis, 0)), lax.ppermute(b, axis, pairs(axis, 1)))


def call(kernel, outs, n_in, scratch, name, space=pltpu.VMEM, limit=VMEM_LIMIT):
    return pl.pallas_call(
        kernel,
        out_shape=outs,
        in_specs=[pl.BlockSpec(memory_space=pltpu.SMEM)] + [pl.BlockSpec(memory_space=space)] * n_in,
        out_specs=jax.tree.map(lambda _: whole(), outs),
        scratch_shapes=scratch,
        compiler_params=pltpu.CompilerParams(vmem_limit_bytes=limit),
        name=name,
    )


def shards(
    velocity,
    stress,
    adj_velocity,
    adj_stress,
    lame_lambda,
    shear_modulus,
    buoyancy,
    gauge_cell,
    gauge_channel,
    gauge_weight,
    channel_angle,
    observed,
):
    owned = observed.shape[1]
    gx = lax.axis_index("gx")
    gy = lax.axis_index("gy")
    par = jnp.stack([gy % 2, gx % 2, (gx - 1) * owned]).astype(jnp.int32)
    slots = (ROWS, 128)
    cell = gauge_cell.reshape(slots)
    chan = gauge_channel.reshape(slots)
    weight = gauge_weight.reshape(slots)
    angle = channel_angle.reshape(16, 128)

    slab = shape((8, 16, 128))
    msg_a, msg_b = call(
        pack_y_kernel,
        (slab, slab),
        5,
        [pltpu.VMEM(f.shape, F32) for f in (stress, velocity, adj_stress, adj_velocity, buoyancy)]
        + [pltpu.SemaphoreType.DMA((Y_GROUPS, 5))],
        "pack_y",
        pltpu.HBM,
        60 * 1024 * 1024,
    )(
        par, stress, velocity, adj_stress, adj_velocity, buoyancy
    )
    ya, yb = swap(msg_a, msg_b, "gy")

    speed = shape((3, 16, 16, 128))
    tensor = shape((6, 16, 16, 128))
    msg = shape((17, MSG_ROWS, 128))
    m_scratch = pltpu.VMEM((3, 20, 16, 128), F32)
    xa, xb, part_v, adj_part_v, edge, adj_edge = call(
        pack_x_kernel,
        (msg, msg, speed, speed, shape((10, 20, 16, 128)), shape((9, 20, 16, 128))),
        8,
        [m_scratch, m_scratch],
        "pack_x",
    )(par, stress, velocity, adj_stress, adj_velocity, buoyancy, angle, ya, yb)
    xa, xb = swap(xa, xb, "gx")
    frame_v, adj_frame_v = pl.pallas_call(
        frame_kernel,
        out_shape=(speed, speed),
        in_specs=[whole()] * 4,
        out_specs=(whole(), whole()),
        compiler_params=pltpu.CompilerParams(vmem_limit_bytes=VMEM_LIMIT),
        name="frame",
    )(stress, adj_stress, edge, adj_edge)

    v_scratch = [pltpu.VMEM((3, 20, 16, 128), F32)] + [pltpu.VMEM((3, 16, 16, 128), F32)] * 2
    buoyancy_edge = edge[9:10]
    velocity_next, stress_next, rates = call(
        functools.partial(step_kernel, 1.0, 0), (speed, tensor, speed), 9, v_scratch, "step"
    )(par, stress, part_v, frame_v, buoyancy, buoyancy_edge, lame_lambda, shear_modulus, xa, xb)

    tile = shape((16, 128))
    part, part_a, part_b, trig = call(
        sample_kernel,
        (tile, tile, tile, shape((3,) + slots)),
        7,
        [
            pltpu.VMEM(slots, jnp.int32),
            pltpu.VMEM((768, 256), BF16),
            pltpu.VMEM((4,) + slots, F32),
            pltpu.VMEM((3,) + slots, F32),
        ],
        "sample",
    )(par, cell, chan, weight, xa, angle, xb, rates.reshape(3, 256, 128))

    part_a, part_b = swap(part_a, part_b, "gx")
    adj_velocity_next, pulled = call(
        functools.partial(step_kernel, -1.0, 8), (speed, tensor), 9, v_scratch, "step_adj"
    )(par, adj_stress, adj_part_v, adj_frame_v, buoyancy, buoyancy_edge, lame_lambda, shear_modulus, xa, xb)

    predicted = part + part_a + part_b
    misfit = predicted - observed.reshape(16, 128)
    robust = misfit / jnp.sqrt(HUBER_SQUARE + misfit * misfit)
    robust_a, robust_b = swap(robust, robust, "gx")

    adj_stress_next = call(
        deposit_kernel,
        shape((6, 256, 128)),
        7,
        [
            pltpu.VMEM(slots, jnp.int32),
            pltpu.VMEM((7,) + slots, F32),
            pltpu.VMEM((256, 768), F32),
        ],
        "deposit",
    )(par, cell, chan, trig, robust_a, robust, robust_b, pulled.reshape(6, 256, 128)).reshape(tensor.shape)
    return (velocity_next, stress_next, predicted.reshape(1, owned), adj_velocity_next, adj_stress_next)


def solution(mesh):
    field = P(None, None, "gx", "gy")
    scalar = P(None, "gx", "gy")
    slot = P("gx", "gy", None)
    row = P("gy", "gx")
    return jax.shard_map(
        shards,
        mesh=mesh,
        in_specs=(field,) * 4 + (scalar,) * 3 + (slot,) * 3 + (row,) * 2,
        out_specs=(field, field, row, field, field),
        check_vma=False,
    )
```

```python
import functools

import jax
import jax.numpy as jnp
from jax import lax
from jax.experimental import pallas as pl
from jax.experimental.pallas import tpu as pltpu
from jax.sharding import PartitionSpec as P

C1 = 9.0 / 8.0
C2 = -1.0 / 24.0
HUBER_SQUARE = 16.0
F32 = jnp.float32
BF16 = jnp.bfloat16
VMEM_LIMIT = 40 * 1024 * 1024

N_Y = 19
EDGE = 3
Y_GROUPS = 2
UNROLL = 16


def whole():
    return pl.BlockSpec(memory_space=pltpu.VMEM)


def shape(dims, dtype=F32):
    return jax.ShapeDtypeStruct(dims, dtype)


def iota(dims, axis):
    return lax.broadcasted_iota(jnp.int32, dims, axis)


def shift_y(f, e, k):
    lane = iota(f.shape, f.ndim - 1)
    n = f.shape[-1]
    if k < 0:
        return pltpu.roll(jnp.where(lane >= n + k, e, f), -k, f.ndim - 1)
    return pltpu.roll(jnp.where(lane < k, e, f), n - k, f.ndim - 1)


def shift_x(f, h, k):
    row = iota(f.shape, f.ndim - 2)
    n = f.shape[-2]
    if k < 0:
        return pltpu.roll(jnp.where(row >= n + k, h, f), -k, f.ndim - 2)
    return pltpu.roll(jnp.where(row < k, h, f), n - k, f.ndim - 2)


def ahead(shift, f, e):
    return C1 * (shift(f, e, 1) - f) + C2 * (shift(f, e, 2) - shift(f, e, -1))


def behind(shift, f, e):
    return C1 * (f - shift(f, e, -1)) + C2 * (shift(f, e, 1) - shift(f, e, -2))


def ahead_z(ref, k, z):
    return C1 * (ref[k, z + 3] - ref[k, z + 2]) + C2 * (ref[k, z + 4] - ref[k, z + 1])


def behind_z(ref, k, z):
    return C1 * (ref[k, z + 2] - ref[k, z + 1]) + C2 * (ref[k, z + 3] - ref[k, z])


def low_half(lane):
    return lane % (2 * EDGE) < EDGE


def pack_y_kernel(s, v, a_s, a_v, b, out_a, out_b, s_ref, v_ref, as_ref, av_ref, b_ref, sems):
    odd = lax.axis_index("gy") % 2 == 1
    hbm = (s, v, a_s, a_v)
    vmem = (s_ref, v_ref, as_ref, av_ref)
    depth = 16 // Y_GROUPS
    copies = []
    for g in range(Y_GROUPS):
        layers = pl.ds(g * depth, depth)
        group = [
            pltpu.make_async_copy(src.at[:, layers], dst.at[:, layers], sems.at[g, i])
            for i, (src, dst) in enumerate(zip(hbm, vmem))
        ]
        group.append(pltpu.make_async_copy(b.at[layers], b_ref.at[layers], sems.at[g, 4]))
        copies.append(group)
        for copy in group:
            copy.start()

    def packed(z):
        lane = iota((16, 128), 1)
        fields = [s_ref[k, z] for k in range(6)] + [v_ref[k, z] for k in range(3)]
        fields += [as_ref[k, z] for k in range(6)] + [av_ref[k, z] for k in range(3)] + [b_ref[z]]
        out = jnp.zeros((16, 128), F32)
        for n, f in enumerate(fields):
            out = jnp.where(lane >= 2 * EDGE * n, pltpu.roll(f, 2 * EDGE * n + EDGE, 1), out)
        return out

    def body(zz, carry):
        low = low_half(iota((16, 128), 1))
        first = packed(2 * zz)
        second = packed(2 * zz + 1)
        up = jnp.where(low, first, pltpu.roll(second, EDGE, 1))
        down = jnp.where(low, pltpu.roll(first, 128 - EDGE, 1), second)
        out_a[zz] = jnp.where(odd, up, down)
        out_b[zz] = jnp.where(odd, down, up)
        return carry

    for g in range(Y_GROUPS):
        for copy in copies[g]:
            copy.wait()
        lax.fori_loop(g * depth // 2, (g + 1) * depth // 2, body, 0, unroll=True)


UP = (0, 7, 4, 5, 6, 8, 12, 13, 14, 1, 2, 3, 9, 10, 11)
DOWN = (1, 2, 7, 3, 6, 9, 10, 11, 14, 0, 4, 5, 8, 12, 13)
PAIRED = 9
MSG_ROWS = 24


def slot(order, item):
    at = order.index(item)
    return 2 * at if at < PAIRED else PAIRED + at


def put_rows(acc, order, item, block, first):
    at = slot(order, item)
    width = 2 if order.index(item) < PAIRED else 1
    src = first if width == 2 or first == 0 else first + 1
    row = iota((8, 128), 0)
    lo = at % 8
    moved = pltpu.roll(block, (lo - src) % 8, 0) if (lo - src) % 8 else block
    acc[at // 8] = jnp.where((row >= lo) & (row < lo + width), moved, acc[at // 8])


def get_rows(msg, order, item, first):
    at = slot(order, item)
    width = 2 if order.index(item) < PAIRED else 1
    src = first if width == 2 or first == 0 else first + 1
    block = msg[8 * (at // 8) : 8 * (at // 8) + 8]
    turn = (src - at % 8) % 8
    return pltpu.roll(block, turn, 0) if turn else block


def pack_x_kernel(s, v, a_s, a_v, b, angle, recv_a, recv_b, out_a, out_b, pv, a_pv, e, a_e, m, a_m):
    odd_y = lax.axis_index("gy") % 2 == 1
    odd_x = lax.axis_index("gx") % 2 == 1
    zero = jnp.zeros((16, 128), F32)
    for ref, n in ((e, 10), (a_e, 9), (m, 3), (a_m, 3)):
        for k in range(n):
            for z in (0, 1, 18, 19):
                ref[k, z] = zero

    def frames(zz, carry):
        low = low_half(iota((16, 128), 1))
        ra = recv_a[zz]
        rb = recv_b[zz]
        before = jnp.where(odd_y, rb, ra)
        after = jnp.where(odd_y, ra, rb)
        both = (
            jnp.where(low, before, pltpu.roll(after, EDGE, 1)),
            jnp.where(low, pltpu.roll(before, 128 - EDGE, 1), after),
        )
        for sub, frame in enumerate(both):
            z = zz * 2 + sub
            for n in range(N_Y):
                value = pltpu.roll(frame, (128 - EDGE - 2 * EDGE * n) % 128, 1)
                if n < 9:
                    e[n, z + 2] = value
                elif n < 18:
                    a_e[n - 9, z + 2] = value
                else:
                    e[9, z + 2] = value
            for k, n in enumerate((2, 4, 5)):
                m[k, z + 2] = s[n, z]
                a_m[k, z + 2] = a_s[n, z]
        return carry

    lax.fori_loop(0, 8, frames, 0, unroll=UNROLL // 2)

    def body(z, carry):
        lane = iota((16, 128), 1)
        by = b[z]
        up = [jnp.zeros((8, 128), F32)] * 3
        down = [jnp.zeros((8, 128), F32)] * 3
        for base, sign, s_ref, v_ref, e_ref, m_ref, out in (
            (0, 1.0, s, v, e, m, pv),
            (8, -1.0, a_s, a_v, a_e, a_m, a_pv),
        ):
            sxx, syy, sxy, sxz, syz = (s_ref[k, z] for k in (0, 1, 3, 4, 5))
            exx, eyy, exy, exz, eyz = (e_ref[k, z + 2] for k in (0, 1, 3, 4, 5))
            cx = ahead(shift_x, sxx, zero) + behind(shift_y, sxy, exy) + behind_z(m_ref, 1, z)
            cy = behind(shift_x, sxy, zero) + ahead(shift_y, syy, eyy) + behind_z(m_ref, 2, z)
            cz = behind(shift_x, sxz, zero) + behind(shift_y, syz, eyz) + ahead_z(m_ref, 0, z)
            ep = jnp.where((lane >= 5) & (lane < 11), pltpu.roll(exy, 8, 1), exx)
            ep = jnp.where((lane >= 13) & (lane < 19), pltpu.roll(exz, 16, 1), ep)
            speeds = [v_ref[k, z] + sign * (by * c) for k, c in enumerate((cx, cy, cz))]
            for k in range(3):
                out[k, z] = speeds[k]
            items = speeds + [sxx, sxy, sxz, ep] + ([by] if base == 0 else [])
            for k, f in enumerate(items):
                put_rows(up, UP, base + k, f[8:16], 6)
                put_rows(down, DOWN, base + k, f[0:8], 0)
        for t in range(3):
            rows = slice(8 * t, 8 * t + 8)
            out_a[z, rows] = jnp.where(odd_x, up[t], down[t])
            out_b[z, rows] = jnp.where(odd_x, down[t], up[t])
        return carry

    lax.fori_loop(0, 16, body, 0, unroll=UNROLL)
    for ref in (out_a, out_b):
        ref[16, 0:16] = angle[...]
        ref[16, 16:24] = jnp.zeros((8, 128), F32)


def frame_kernel(s, a_s, e, a_e, out, a_out):
    zero = jnp.zeros((16, 128), F32)

    def body(z, carry):
        be = e[9, z + 2]
        for sign, s_ref, e_ref, o in ((1.0, s, e, out), (-1.0, a_s, a_e, a_out)):
            syy, sxy, syz = (s_ref[k, z] for k in (1, 3, 5))
            exx, eyy, exy, exz, eyz = (e_ref[k, z + 2] for k in (0, 1, 3, 4, 5))
            cx = ahead(shift_x, exx, zero) + behind(shift_y, exy, sxy) + behind_z(e_ref, 4, z)
            cy = behind(shift_x, exy, zero) + ahead(shift_y, eyy, syy) + behind_z(e_ref, 5, z)
            cz = behind(shift_x, exz, zero) + behind(shift_y, eyz, syz) + ahead_z(e_ref, 2, z)
            for k, c in enumerate((cx, cy, cz)):
                o[k, z] = e_ref[6 + k, z + 2] + sign * (be * c)
        return carry

    lax.fori_loop(0, 16, body, 0, unroll=UNROLL)


def masked_roll(block, k, low, high):
    row = iota((8, 128), 0)
    return jnp.where((row >= low) & (row < high), pltpu.roll(block, k % 8, 0), 0.0)


def ahead_first(block):
    return -C2 * masked_roll(block, 1, 0, 1)


def ahead_last(block):
    return C1 * masked_roll(block, -1, 7, 8) + C2 * masked_roll(block, -2, 6, 8)


def behind_first(block):
    return -C1 * masked_roll(block, 1, 0, 1) - C2 * masked_roll(block, 2, 0, 2)


def behind_last(block):
    return C2 * masked_roll(block, -1, 7, 8)


ADDED = ((ahead_first, ahead_last), (behind_first, behind_last), (behind_first, behind_last))


def step_kernel(sign, base, s, pv, pve, b, be, lam, mu, recv_a, recv_b, v_out, s_out, *rest):
    r_out = rest[0] if len(rest) == 4 else None
    vm_ref, ve_ref, vh_ref = rest[-3:]
    odd_x = lax.axis_index("gx") % 2 == 1
    zero = jnp.zeros((16, 128), F32)
    for k in range(3):
        for z in (0, 1, 18, 19):
            vm_ref[k, z] = zero

    def speeds(z, carry):
        xa = recv_a[z]
        xb = recv_b[z]
        before = jnp.where(odd_x, xb, xa)
        after = jnp.where(odd_x, xa, xb)

        def halo(item):
            return (get_rows(before, UP, item, 6), get_rows(after, DOWN, item, 0))

        b_left, b_right = halo(7)
        p_left, p_right = halo(base + 6)
        by = b[z]
        bf = be[0, z + 2]
        for k, (first, last) in enumerate(ADDED):
            left, right = halo(base + 3 + k)
            new = pv[k, z] + sign * (by * jnp.concatenate([first(left), last(right)], axis=0))
            vm_ref[k, z + 2] = new
            v_out[k, z] = new
            turn = (128 - 8 * k) % 128
            e_left = pltpu.roll(p_left, turn, 1) if turn else p_left
            e_right = pltpu.roll(p_right, turn, 1) if turn else p_right
            ve_ref[k, z] = pve[k, z] + sign * (bf * jnp.concatenate([first(e_left), last(e_right)], axis=0))
            v_left, v_right = halo(base + k)
            f = s[(0, 3, 4)[k], z]
            vh_ref[k, z, 0:8] = v_right + sign * (b_right * first(f[8:16]))
            vh_ref[k, z, 8:16] = v_left + sign * (b_left * last(f[0:8]))
        return carry

    lax.fori_loop(0, 16, speeds, 0, unroll=UNROLL)

    def rates(z, carry):
        vx, vy, vz = (vm_ref[k, z + 2] for k in range(3))
        ex, ey, ez = (ve_ref[k, z] for k in range(3))
        hx, hy, hz = (vh_ref[k, z] for k in range(3))
        r0 = behind(shift_x, vx, hx)
        r1 = behind(shift_y, vy, ey)
        r2 = behind_z(vm_ref, 2, z)
        r3 = ahead(shift_y, vx, ex) + ahead(shift_x, vy, hy)
        r4 = ahead_z(vm_ref, 0, z) + ahead(shift_x, vz, hz)
        r5 = ahead_z(vm_ref, 1, z) + ahead(shift_y, vz, ez)
        m = mu[z]
        volume = lam[z] * (r0 + r1 + r2)
        m2 = 2.0 * m
        for k, c in enumerate((volume + m2 * r0, volume + m2 * r1, volume + m2 * r2, m * r3, m * r4, m * r5)):
            s_out[k, z] = s[k, z] + sign * c
        if r_out is not None:
            r_out[0, z] = r0
            r_out[1, z] = r1
            r_out[2, z] = r3
        return carry

    lax.fori_loop(0, 16, rates, 0, unroll=UNROLL)


CHUNK = 8192
TILE = CHUNK // 128
ROWS = 64
OWNED = 2048


def pieces(x, n):
    out = []
    for _ in range(n):
        p = x.astype(BF16)
        out.append(p)
        x = x - p.astype(F32)
    return out


def lanes_of(ref, q):
    return jnp.concatenate([ref[pl.ds(q * TILE + i, 1), :] for i in range(TILE)], axis=1)


def put_lanes(ref, k, q, row):
    for i in range(TILE):
        ref[k, pl.ds(q * TILE + i, 1), :] = row[:, 128 * i : 128 * (i + 1)]


def one_hot(index, n):
    return (iota((n, index.shape[1]), 0) == index).astype(F32).astype(BF16)


def pick(out, low, n):
    acc = jnp.zeros((8, out.shape[1]), F32)
    for t in range(n // 8):
        hit = iota(acc.shape, 0) + 8 * t == low
        acc = acc + jnp.where(hit, out[8 * t : 8 * t + 8], 0.0)
    return jnp.sum(acc, axis=0, keepdims=True)


def dot(a, b):
    return jnp.dot(a, b, preferred_element_type=F32)


def dot_nt(a, b):
    return lax.dot_general(a, b, (((1,), (1,)), ((), ())), preferred_element_type=F32)


def pick_channel(q, table, chan):
    c = lanes_of(chan, q)
    high = one_hot(c >> 7, 48)
    out = dot(table, jnp.concatenate([high] * 3, axis=0))
    return pick(out, c & 127, 128)


def channel_table(rows):
    return jnp.concatenate(pieces(rows.T, 3), axis=1)


def sample_kernel(
    cell, chan_raw, weight, recv_a, angle, recv_b, rates, part, part_a, part_b, trig, chan, table, rows, vals
):
    chan[...] = chan_raw[...] - (lax.axis_index("gx") - 1) * OWNED
    odd_x = lax.axis_index("gx") % 2 == 1
    aa = recv_a[16, 0:16]
    ab = recv_b[16, 0:16]
    angles = jnp.concatenate([jnp.where(odd_x, ab, aa), angle[...], jnp.where(odd_x, aa, ab)], axis=0)
    ang = channel_table(angles)
    for k in range(3):
        hi, lo = pieces(rates[k].T, 2)
        table[128 * k : 128 * (k + 1)] = hi
        table[384 + 128 * k : 384 + 128 * (k + 1)] = lo

    def gather(q, carry):
        put_lanes(rows, 0, q, pick_channel(q, ang, chan))
        c = lanes_of(cell, q)
        out = dot(table[...], one_hot(c >> 7, 256))
        low = c & 127
        for k in range(3):
            both = out[128 * k : 128 * (k + 1)] + out[384 + 128 * k : 384 + 128 * (k + 1)]
            put_lanes(rows, 1 + k, q, pick(both, low, 128))
        return carry

    lax.fori_loop(0, 8192 // CHUNK, gather, 0)
    theta = rows[0]
    cosine = jnp.cos(theta)
    sine = jnp.sin(theta)
    w = weight[...]
    t0 = w * (cosine * cosine)
    t1 = w * (sine * sine)
    t2 = w * (cosine * sine)
    trig[0] = t0
    trig[1] = t1
    trig[2] = t2
    value = t0 * rows[1] + t1 * rows[2] + t2 * rows[3]
    for k, p in enumerate(pieces(value, 3)):
        vals[k] = p.astype(F32)

    def scatter(q, acc):
        c = lanes_of(chan, q)
        hit = iota((48, CHUNK), 0) == c >> 7
        a = jnp.concatenate([jnp.where(hit, lanes_of(vals.at[k], q), 0.0) for k in range(3)], axis=0)
        return acc + dot_nt(a.astype(BF16), one_hot(c & 127, 128))

    acc = lax.fori_loop(0, 8192 // CHUNK, scatter, jnp.zeros((144, 128), F32))
    total = acc[0:48] + acc[48:96] + acc[96:144]
    part[...] = total[16:32]
    part_a[...] = jnp.where(odd_x, total[32:48], total[0:16])
    part_b[...] = jnp.where(odd_x, total[0:16], total[32:48])


def deposit_kernel(cell, chan_raw, trig, robust_a, robust, robust_b, pulled, out, chan, vals, acc):
    chan[...] = chan_raw[...] - (lax.axis_index("gx") - 1) * OWNED
    odd_x = lax.axis_index("gx") % 2 == 1
    ra = robust_a[...]
    rb = robust_b[...]
    tab = channel_table(
        jnp.concatenate([jnp.where(odd_x, rb, ra), robust[...], jnp.where(odd_x, ra, rb)], axis=0)
    )

    def gather(q, carry):
        put_lanes(vals, 6, q, pick_channel(q, tab, chan))
        return carry

    lax.fori_loop(0, 8192 // CHUNK, gather, 0)
    rob = vals[6]
    for k in range(3):
        for i, p in enumerate(pieces(trig[k] * rob, 2)):
            vals[2 * k + i] = p.astype(F32)
    acc[...] = jnp.zeros(acc.shape, F32)

    def place(q, carry):
        c = lanes_of(cell, q)
        hit = iota((128, CHUNK), 0) == c & 127
        b = jnp.concatenate([jnp.where(hit, lanes_of(vals.at[k], q), 0.0).astype(BF16) for k in range(6)], axis=0)
        acc[...] += dot_nt(b, one_hot(c >> 7, 256))
        return carry

    lax.fori_loop(0, 8192 // CHUNK, place, 0)
    for k in (2, 4, 5):
        out[k] = pulled[k]
    for n, k in enumerate((0, 1, 3)):
        both = acc[256 * n : 256 * n + 128] + acc[256 * n + 128 : 256 * n + 256]
        out[k] = pulled[k] + both.T


def pairs(axis, first):
    size = lax.axis_size(axis)
    route = []
    for i in range(first, size - 1, 2):
        route += [(i, i + 1), (i + 1, i)]
    return route


def swap(a, b, axis):
    return (lax.ppermute(a, axis, pairs(axis, 1)), lax.ppermute(b, axis, pairs(axis, 0)))


def call(kernel, outs, n_in, scratch, name, space=pltpu.VMEM, limit=VMEM_LIMIT):
    return pl.pallas_call(
        kernel,
        out_shape=outs,
        in_specs=[pl.BlockSpec(memory_space=space)] * n_in,
        out_specs=jax.tree.map(lambda _: whole(), outs),
        scratch_shapes=scratch,
        compiler_params=pltpu.CompilerParams(vmem_limit_bytes=limit),
        name=name,
    )


def shards(
    velocity,
    stress,
    adj_velocity,
    adj_stress,
    lame_lambda,
    shear_modulus,
    buoyancy,
    gauge_cell,
    gauge_channel,
    gauge_weight,
    channel_angle,
    observed,
):
    owned = observed.shape[1]
    slots = (ROWS, 128)
    cell = gauge_cell.reshape(slots)
    chan = gauge_channel.reshape(slots)
    weight = gauge_weight.reshape(slots)
    angle = channel_angle.reshape(16, 128)

    slab = shape((8, 16, 128))
    msg_a, msg_b = call(
        pack_y_kernel,
        (slab, slab),
        5,
        [pltpu.VMEM(f.shape, F32) for f in (stress, velocity, adj_stress, adj_velocity, buoyancy)]
        + [pltpu.SemaphoreType.DMA((Y_GROUPS, 5))],
        "pack_y",
        pltpu.HBM,
        60 * 1024 * 1024,
    )(
        stress, velocity, adj_stress, adj_velocity, buoyancy
    )
    ya, yb = swap(msg_a, msg_b, "gy")

    speed = shape((3, 16, 16, 128))
    tensor = shape((6, 16, 16, 128))
    msg = shape((17, MSG_ROWS, 128))
    m_scratch = pltpu.VMEM((3, 20, 16, 128), F32)
    xa, xb, part_v, adj_part_v, edge, adj_edge = call(
        pack_x_kernel,
        (msg, msg, speed, speed, shape((10, 20, 16, 128)), shape((9, 20, 16, 128))),
        8,
        [m_scratch, m_scratch],
        "pack_x",
    )(stress, velocity, adj_stress, adj_velocity, buoyancy, angle, ya, yb)
    xa, xb = swap(xa, xb, "gx")
    frame_v, adj_frame_v = pl.pallas_call(
        frame_kernel,
        out_shape=(speed, speed),
        in_specs=[whole()] * 4,
        out_specs=(whole(), whole()),
        compiler_params=pltpu.CompilerParams(vmem_limit_bytes=VMEM_LIMIT),
        name="frame",
    )(stress, adj_stress, edge, adj_edge)

    v_scratch = [pltpu.VMEM((3, 20, 16, 128), F32)] + [pltpu.VMEM((3, 16, 16, 128), F32)] * 2
    buoyancy_edge = edge[9:10]
    velocity_next, stress_next, rates = call(
        functools.partial(step_kernel, 1.0, 0), (speed, tensor, speed), 9, v_scratch, "step"
    )(stress, part_v, frame_v, buoyancy, buoyancy_edge, lame_lambda, shear_modulus, xa, xb)

    tile = shape((16, 128))
    part, part_a, part_b, trig = call(
        sample_kernel,
        (tile, tile, tile, shape((3,) + slots)),
        7,
        [
            pltpu.VMEM(slots, jnp.int32),
            pltpu.VMEM((768, 256), BF16),
            pltpu.VMEM((4,) + slots, F32),
            pltpu.VMEM((3,) + slots, F32),
        ],
        "sample",
    )(cell, chan, weight, xa, angle, xb, rates.reshape(3, 256, 128))

    part_a, part_b = swap(part_a, part_b, "gx")
    adj_velocity_next, pulled = call(
        functools.partial(step_kernel, -1.0, 8), (speed, tensor), 9, v_scratch, "step_adj"
    )(adj_stress, adj_part_v, adj_frame_v, buoyancy, buoyancy_edge, lame_lambda, shear_modulus, xa, xb)

    predicted = part + part_a + part_b
    misfit = predicted - observed.reshape(16, 128)
    robust = misfit / jnp.sqrt(HUBER_SQUARE + misfit * misfit)
    robust_a, robust_b = swap(robust, robust, "gx")

    adj_stress_next = call(
        deposit_kernel,
        shape((6, 256, 128)),
        7,
        [
            pltpu.VMEM(slots, jnp.int32),
            pltpu.VMEM((7,) + slots, F32),
            pltpu.VMEM((768, 256), F32),
        ],
        "deposit",
    )(cell, chan, trig, robust_a, robust, robust_b, pulled.reshape(6, 256, 128)).reshape(tensor.shape)
    return (velocity_next, stress_next, predicted.reshape(1, owned), adj_velocity_next, adj_stress_next)


def solution(mesh):
    field = P(None, None, "gx", "gy")
    scalar = P(None, "gx", "gy")
    slot = P("gx", "gy", None)
    row = P("gy", "gx")
    return jax.shard_map(
        shards,
        mesh=mesh,
        in_specs=(field,) * 4 + (scalar,) * 3 + (slot,) * 3 + (row,) * 2,
        out_specs=(field, field, row, field, field),
        check_vma=False,
    )
```

```python
import functools

import jax
import jax.numpy as jnp
from jax import lax
from jax.experimental import pallas as pl
from jax.experimental.pallas import tpu as pltpu
from jax.sharding import PartitionSpec as P

C1 = 9.0 / 8.0
C2 = -1.0 / 24.0
HUBER_SQUARE = 16.0
F32 = jnp.float32
BF16 = jnp.bfloat16
VMEM_LIMIT = 40 * 1024 * 1024
PACK_LIMIT = 53 * 1024 * 1024 + 768 * 1024

N_Y = 19
EDGE = 3
Y_GROUPS = 2
UNROLL = 16


def whole():
    return pl.BlockSpec(memory_space=pltpu.VMEM)


def shape(dims, dtype=F32):
    return jax.ShapeDtypeStruct(dims, dtype)


def iota(dims, axis):
    return lax.broadcasted_iota(jnp.int32, dims, axis)


def shift_y(f, e, k):
    lane = iota(f.shape, f.ndim - 1)
    n = f.shape[-1]
    if k < 0:
        return pltpu.roll(jnp.where(lane >= n + k, e, f), -k, f.ndim - 1)
    return pltpu.roll(jnp.where(lane < k, e, f), n - k, f.ndim - 1)


def shift_x(f, h, k):
    row = iota(f.shape, f.ndim - 2)
    n = f.shape[-2]
    if k < 0:
        return pltpu.roll(jnp.where(row >= n + k, h, f), -k, f.ndim - 2)
    return pltpu.roll(jnp.where(row < k, h, f), n - k, f.ndim - 2)


def ahead(shift, f, e):
    return C1 * (shift(f, e, 1) - f) + C2 * (shift(f, e, 2) - shift(f, e, -1))


def behind(shift, f, e):
    return C1 * (f - shift(f, e, -1)) + C2 * (shift(f, e, 1) - shift(f, e, -2))


def ahead_z(ref, k, z):
    return C1 * (ref[k, z + 3] - ref[k, z + 2]) + C2 * (ref[k, z + 4] - ref[k, z + 1])


def behind_z(ref, k, z):
    return C1 * (ref[k, z + 2] - ref[k, z + 1]) + C2 * (ref[k, z + 3] - ref[k, z])


def low_half(lane):
    return lane % (2 * EDGE) < EDGE


def pack_y_kernel(s, v, a_s, a_v, b, out_a, out_b, s_ref, v_ref, as_ref, av_ref, b_ref, sems):
    odd = lax.axis_index("gy") % 2 == 1
    hbm = (s, v, a_s, a_v)
    vmem = (s_ref, v_ref, as_ref, av_ref)
    depth = 16 // Y_GROUPS
    copies = []
    for g in range(Y_GROUPS):
        layers = pl.ds(g * depth, depth)
        group = [
            pltpu.make_async_copy(src.at[:, layers], dst.at[:, layers], sems.at[g, i])
            for i, (src, dst) in enumerate(zip(hbm, vmem))
        ]
        group.append(pltpu.make_async_copy(b.at[layers], b_ref.at[layers], sems.at[g, 4]))
        copies.append(group)
        for copy in group:
            copy.start()

    def packed(z):
        lane = iota((16, 128), 1)
        fields = [s_ref[k, z] for k in range(6)] + [v_ref[k, z] for k in range(3)]
        fields += [as_ref[k, z] for k in range(6)] + [av_ref[k, z] for k in range(3)] + [b_ref[z]]
        out = jnp.zeros((16, 128), F32)
        for n, f in enumerate(fields):
            out = jnp.where(lane >= 2 * EDGE * n, pltpu.roll(f, 2 * EDGE * n + EDGE, 1), out)
        return out

    def body(zz, carry):
        low = low_half(iota((16, 128), 1))
        first = packed(2 * zz)
        second = packed(2 * zz + 1)
        up = jnp.where(low, first, pltpu.roll(second, EDGE, 1))
        down = jnp.where(low, pltpu.roll(first, 128 - EDGE, 1), second)
        out_a[zz] = jnp.where(odd, up, down)
        out_b[zz] = jnp.where(odd, down, up)
        return carry

    for g in range(Y_GROUPS):
        for copy in copies[g]:
            copy.wait()
        lax.fori_loop(g * depth // 2, (g + 1) * depth // 2, body, 0, unroll=True)


UP = (0, 7, 4, 5, 6, 8, 12, 13, 14, 1, 2, 3, 9, 10, 11)
DOWN = (1, 2, 7, 3, 6, 9, 10, 11, 14, 0, 4, 5, 8, 12, 13)
PAIRED = 9
MSG_ROWS = 24


def slot(order, item):
    at = order.index(item)
    return 2 * at if at < PAIRED else PAIRED + at


def put_rows(acc, order, item, block, first):
    at = slot(order, item)
    width = 2 if order.index(item) < PAIRED else 1
    src = first if width == 2 or first == 0 else first + 1
    row = iota((8, 128), 0)
    lo = at % 8
    moved = pltpu.roll(block, (lo - src) % 8, 0) if (lo - src) % 8 else block
    acc[at // 8] = jnp.where((row >= lo) & (row < lo + width), moved, acc[at // 8])


def get_rows(msg, order, item, first):
    at = slot(order, item)
    width = 2 if order.index(item) < PAIRED else 1
    src = first if width == 2 or first == 0 else first + 1
    block = msg[8 * (at // 8) : 8 * (at // 8) + 8]
    turn = (src - at % 8) % 8
    return pltpu.roll(block, turn, 0) if turn else block


def pack_x_kernel(s, v, a_s, a_v, b, recv_a, recv_b, angle, out_a, out_b, pv, a_pv, e, a_e, m, a_m):
    odd_y = lax.axis_index("gy") % 2 == 1
    odd_x = lax.axis_index("gx") % 2 == 1
    zero = jnp.zeros((16, 128), F32)
    for ref, n in ((e, 10), (a_e, 9), (m, 3), (a_m, 3)):
        for k in range(n):
            for z in (0, 1, 18, 19):
                ref[k, z] = zero

    def frames(zz, carry):
        low = low_half(iota((16, 128), 1))
        ra = recv_a[zz]
        rb = recv_b[zz]
        before = jnp.where(odd_y, rb, ra)
        after = jnp.where(odd_y, ra, rb)
        both = (
            jnp.where(low, before, pltpu.roll(after, EDGE, 1)),
            jnp.where(low, pltpu.roll(before, 128 - EDGE, 1), after),
        )
        for sub, frame in enumerate(both):
            z = zz * 2 + sub
            for n in range(N_Y):
                value = pltpu.roll(frame, (128 - EDGE - 2 * EDGE * n) % 128, 1)
                if n < 9:
                    e[n, z + 2] = value
                elif n < 18:
                    a_e[n - 9, z + 2] = value
                else:
                    e[9, z + 2] = value
            for k, n in enumerate((2, 4, 5)):
                m[k, z + 2] = s[n, z]
                a_m[k, z + 2] = a_s[n, z]
        return carry

    lax.fori_loop(0, 8, frames, 0, unroll=UNROLL // 2)

    def body(z, carry):
        lane = iota((16, 128), 1)
        by = b[z]
        up = [jnp.zeros((8, 128), F32)] * 3
        down = [jnp.zeros((8, 128), F32)] * 3
        for base, sign, s_ref, v_ref, e_ref, m_ref, out in (
            (0, 1.0, s, v, e, m, pv),
            (8, -1.0, a_s, a_v, a_e, a_m, a_pv),
        ):
            sxx, syy, sxy, sxz, syz = (s_ref[k, z] for k in (0, 1, 3, 4, 5))
            exx, eyy, exy, exz, eyz = (e_ref[k, z + 2] for k in (0, 1, 3, 4, 5))
            cx = ahead(shift_x, sxx, zero) + behind(shift_y, sxy, exy) + behind_z(m_ref, 1, z)
            cy = behind(shift_x, sxy, zero) + ahead(shift_y, syy, eyy) + behind_z(m_ref, 2, z)
            cz = behind(shift_x, sxz, zero) + behind(shift_y, syz, eyz) + ahead_z(m_ref, 0, z)
            ep = jnp.where((lane >= 5) & (lane < 11), pltpu.roll(exy, 8, 1), exx)
            ep = jnp.where((lane >= 13) & (lane < 19), pltpu.roll(exz, 16, 1), ep)
            speeds = [v_ref[k, z] + sign * (by * c) for k, c in enumerate((cx, cy, cz))]
            for k in range(3):
                out[k, z] = speeds[k]
            items = speeds + [sxx, sxy, sxz, ep] + ([by] if base == 0 else [])
            for k, f in enumerate(items):
                put_rows(up, UP, base + k, f[8:16], 6)
                put_rows(down, DOWN, base + k, f[0:8], 0)
        for t in range(3):
            rows = slice(8 * t, 8 * t + 8)
            out_a[z, rows] = jnp.where(odd_x, up[t], down[t])
            out_b[z, rows] = jnp.where(odd_x, down[t], up[t])
        return carry

    lax.fori_loop(0, 16, body, 0, unroll=UNROLL)
    for ref in (out_a, out_b):
        ref[16, 0:16] = angle[...]
        ref[16, 16:24] = jnp.zeros((8, 128), F32)


def frame_kernel(s, a_s, e, a_e, out, a_out):
    zero = jnp.zeros((16, 128), F32)

    def body(z, carry):
        be = e[9, z + 2]
        for sign, s_ref, e_ref, o in ((1.0, s, e, out), (-1.0, a_s, a_e, a_out)):
            syy, sxy, syz = (s_ref[k, z] for k in (1, 3, 5))
            exx, eyy, exy, exz, eyz = (e_ref[k, z + 2] for k in (0, 1, 3, 4, 5))
            cx = ahead(shift_x, exx, zero) + behind(shift_y, exy, sxy) + behind_z(e_ref, 4, z)
            cy = behind(shift_x, exy, zero) + ahead(shift_y, eyy, syy) + behind_z(e_ref, 5, z)
            cz = behind(shift_x, exz, zero) + behind(shift_y, eyz, syz) + ahead_z(e_ref, 2, z)
            for k, c in enumerate((cx, cy, cz)):
                o[k, z] = e_ref[6 + k, z + 2] + sign * (be * c)
        return carry

    lax.fori_loop(0, 16, body, 0, unroll=UNROLL)


def masked_roll(block, k, low, high):
    row = iota((8, 128), 0)
    return jnp.where((row >= low) & (row < high), pltpu.roll(block, k % 8, 0), 0.0)


def ahead_first(block):
    return -C2 * masked_roll(block, 1, 0, 1)


def ahead_last(block):
    return C1 * masked_roll(block, -1, 7, 8) + C2 * masked_roll(block, -2, 6, 8)


def behind_first(block):
    return -C1 * masked_roll(block, 1, 0, 1) - C2 * masked_roll(block, 2, 0, 2)


def behind_last(block):
    return C2 * masked_roll(block, -1, 7, 8)


ADDED = ((ahead_first, ahead_last), (behind_first, behind_last), (behind_first, behind_last))


def step_kernel(sign, base, s, pv, pve, b, be, lam, mu, recv_a, recv_b, v_out, s_out, *rest):
    r_out = rest[0] if len(rest) == 4 else None
    vm_ref, ve_ref, vh_ref = rest[-3:]
    odd_x = lax.axis_index("gx") % 2 == 1
    zero = jnp.zeros((16, 128), F32)
    for k in range(3):
        for z in (0, 1, 18, 19):
            vm_ref[k, z] = zero

    def speeds(z, carry):
        xa = recv_a[z]
        xb = recv_b[z]
        before = jnp.where(odd_x, xb, xa)
        after = jnp.where(odd_x, xa, xb)

        def halo(item):
            return (get_rows(before, UP, item, 6), get_rows(after, DOWN, item, 0))

        b_left, b_right = halo(7)
        p_left, p_right = halo(base + 6)
        by = b[z]
        bf = be[0, z + 2]
        for k, (first, last) in enumerate(ADDED):
            left, right = halo(base + 3 + k)
            new = pv[k, z] + sign * (by * jnp.concatenate([first(left), last(right)], axis=0))
            vm_ref[k, z + 2] = new
            v_out[k, z] = new
            turn = (128 - 8 * k) % 128
            e_left = pltpu.roll(p_left, turn, 1) if turn else p_left
            e_right = pltpu.roll(p_right, turn, 1) if turn else p_right
            ve_ref[k, z] = pve[k, z] + sign * (bf * jnp.concatenate([first(e_left), last(e_right)], axis=0))
            v_left, v_right = halo(base + k)
            f = s[(0, 3, 4)[k], z]
            vh_ref[k, z, 0:8] = v_right + sign * (b_right * first(f[8:16]))
            vh_ref[k, z, 8:16] = v_left + sign * (b_left * last(f[0:8]))
        return carry

    lax.fori_loop(0, 16, speeds, 0, unroll=UNROLL)

    def rates(z, carry):
        vx, vy, vz = (vm_ref[k, z + 2] for k in range(3))
        ex, ey, ez = (ve_ref[k, z] for k in range(3))
        hx, hy, hz = (vh_ref[k, z] for k in range(3))
        r0 = behind(shift_x, vx, hx)
        r1 = behind(shift_y, vy, ey)
        r2 = behind_z(vm_ref, 2, z)
        r3 = ahead(shift_y, vx, ex) + ahead(shift_x, vy, hy)
        r4 = ahead_z(vm_ref, 0, z) + ahead(shift_x, vz, hz)
        r5 = ahead_z(vm_ref, 1, z) + ahead(shift_y, vz, ez)
        m = mu[z]
        volume = lam[z] * (r0 + r1 + r2)
        m2 = 2.0 * m
        for k, c in enumerate((volume + m2 * r0, volume + m2 * r1, volume + m2 * r2, m * r3, m * r4, m * r5)):
            s_out[k, z] = s[k, z] + sign * c
        if r_out is not None:
            r_out[0, z] = r0
            r_out[1, z] = r1
            r_out[2, z] = r3
        return carry

    lax.fori_loop(0, 16, rates, 0, unroll=UNROLL)


CHUNK = 8192
TILE = CHUNK // 128
ROWS = 64
OWNED = 2048


def pieces(x, n):
    out = []
    for _ in range(n):
        p = x.astype(BF16)
        out.append(p)
        x = x - p.astype(F32)
    return out


def lanes_of(ref, q):
    return jnp.concatenate([ref[pl.ds(q * TILE + i, 1), :] for i in range(TILE)], axis=1)


def put_lanes(ref, k, q, row):
    for i in range(TILE):
        ref[k, pl.ds(q * TILE + i, 1), :] = row[:, 128 * i : 128 * (i + 1)]


def one_hot(index, n):
    return (iota((n, index.shape[1]), 0) == index).astype(F32).astype(BF16)


def pick(out, low, n):
    acc = jnp.zeros((8, out.shape[1]), F32)
    for t in range(n // 8):
        hit = iota(acc.shape, 0) + 8 * t == low
        acc = acc + jnp.where(hit, out[8 * t : 8 * t + 8], 0.0)
    return jnp.sum(acc, axis=0, keepdims=True)


def dot(a, b):
    return jnp.dot(a, b, preferred_element_type=F32)


def dot_nt(a, b):
    return lax.dot_general(a, b, (((1,), (1,)), ((), ())), preferred_element_type=F32)


def pick_channel(q, table, chan):
    c = lanes_of(chan, q)
    high = one_hot(c >> 7, 48)
    out = dot(table, jnp.concatenate([high] * 3, axis=0))
    return pick(out, c & 127, 128)


def channel_table(rows):
    return jnp.concatenate(pieces(rows.T, 3), axis=1)


def sample_kernel(
    cell, chan_raw, weight, recv_a, angle, recv_b, rates, part, part_a, part_b, trig, chan, table, rows, vals
):
    chan[...] = chan_raw[...] - (lax.axis_index("gx") - 1) * OWNED
    odd_x = lax.axis_index("gx") % 2 == 1
    aa = recv_a[16, 0:16]
    ab = recv_b[16, 0:16]
    angles = jnp.concatenate([jnp.where(odd_x, ab, aa), angle[...], jnp.where(odd_x, aa, ab)], axis=0)
    ang = channel_table(angles)
    for k in range(3):
        hi, lo = pieces(rates[k].reshape(256, 128).T, 2)
        table[128 * k : 128 * (k + 1)] = hi
        table[384 + 128 * k : 384 + 128 * (k + 1)] = lo

    def gather(q, carry):
        put_lanes(rows, 0, q, pick_channel(q, ang, chan))
        c = lanes_of(cell, q)
        out = dot(table[...], one_hot(c >> 7, 256))
        low = c & 127
        for k in range(3):
            both = out[128 * k : 128 * (k + 1)] + out[384 + 128 * k : 384 + 128 * (k + 1)]
            put_lanes(rows, 1 + k, q, pick(both, low, 128))
        return carry

    lax.fori_loop(0, 8192 // CHUNK, gather, 0)
    theta = rows[0]
    cosine = jnp.cos(theta)
    sine = jnp.sin(theta)
    w = weight[...]
    t0 = w * (cosine * cosine)
    t1 = w * (sine * sine)
    t2 = w * (cosine * sine)
    trig[0] = t0
    trig[1] = t1
    trig[2] = t2
    value = t0 * rows[1] + t1 * rows[2] + t2 * rows[3]
    for k, p in enumerate(pieces(value, 3)):
        vals[k] = p.astype(F32)

    def scatter(q, acc):
        c = lanes_of(chan, q)
        hit = iota((48, CHUNK), 0) == c >> 7
        a = jnp.concatenate([jnp.where(hit, lanes_of(vals.at[k], q), 0.0) for k in range(3)], axis=0)
        return acc + dot_nt(a.astype(BF16), one_hot(c & 127, 128))

    acc = lax.fori_loop(0, 8192 // CHUNK, scatter, jnp.zeros((144, 128), F32))
    total = acc[0:48] + acc[48:96] + acc[96:144]
    part[...] = total[16:32]
    part_a[...] = jnp.where(odd_x, total[32:48], total[0:16])
    part_b[...] = jnp.where(odd_x, total[0:16], total[32:48])


def forward_kernel(*refs):
    fields, gauges, outs, scratch = refs[:9], refs[9:13], refs[13:19], refs[19:]
    speeds, rates, slots = scratch[:3], scratch[3], scratch[4:]
    step_kernel(1.0, 0, *fields, *outs[:2], rates, *speeds)
    cell, chan, weight, angle = gauges
    sample_kernel(cell, chan, weight, fields[7], angle, fields[8], rates, *outs[2:], *slots)


def deposit_kernel(cell, chan_raw, trig, robust_a, robust, robust_b, pulled, out, chan, vals, acc):
    chan[...] = chan_raw[...] - (lax.axis_index("gx") - 1) * OWNED
    odd_x = lax.axis_index("gx") % 2 == 1
    ra = robust_a[...]
    rb = robust_b[...]
    tab = channel_table(
        jnp.concatenate([jnp.where(odd_x, rb, ra), robust[...], jnp.where(odd_x, ra, rb)], axis=0)
    )

    def gather(q, carry):
        put_lanes(vals, 6, q, pick_channel(q, tab, chan))
        return carry

    lax.fori_loop(0, 8192 // CHUNK, gather, 0)
    rob = vals[6]
    for k in range(3):
        for i, p in enumerate(pieces(trig[k] * rob, 2)):
            vals[2 * k + i] = p.astype(F32)
    acc[...] = jnp.zeros(acc.shape, F32)

    def place(q, carry):
        c = lanes_of(cell, q)
        hit = iota((128, CHUNK), 0) == c & 127
        b = jnp.concatenate([jnp.where(hit, lanes_of(vals.at[k], q), 0.0).astype(BF16) for k in range(6)], axis=0)
        acc[...] += dot_nt(b, one_hot(c >> 7, 256))
        return carry

    lax.fori_loop(0, 8192 // CHUNK, place, 0)
    for k in (2, 4, 5):
        out[k] = pulled[k]
    for n, k in enumerate((0, 1, 3)):
        both = acc[256 * n : 256 * n + 128] + acc[256 * n + 128 : 256 * n + 256]
        out[k] = pulled[k] + both.T


def pairs(axis, first):
    size = lax.axis_size(axis)
    route = []
    for i in range(first, size - 1, 2):
        route += [(i, i + 1), (i + 1, i)]
    return route


def swap(a, b, axis):
    return (lax.ppermute(a, axis, pairs(axis, 1)), lax.ppermute(b, axis, pairs(axis, 0)))


def call(kernel, outs, n_in, scratch, name, space=pltpu.VMEM, limit=VMEM_LIMIT):
    return pl.pallas_call(
        kernel,
        out_shape=outs,
        in_specs=[pl.BlockSpec(memory_space=space)] * n_in,
        out_specs=jax.tree.map(lambda _: whole(), outs),
        scratch_shapes=scratch,
        compiler_params=pltpu.CompilerParams(vmem_limit_bytes=limit),
        name=name,
    )


def shards(
    velocity,
    stress,
    adj_velocity,
    adj_stress,
    lame_lambda,
    shear_modulus,
    buoyancy,
    gauge_cell,
    gauge_channel,
    gauge_weight,
    channel_angle,
    observed,
):
    owned = observed.shape[1]
    slots = (ROWS, 128)
    cell = gauge_cell.reshape(slots)
    chan = gauge_channel.reshape(slots)
    weight = gauge_weight.reshape(slots)
    angle = channel_angle.reshape(16, 128)

    slab = shape((8, 16, 128))
    msg_a, msg_b = call(
        pack_y_kernel,
        (slab, slab),
        5,
        [pltpu.VMEM(f.shape, F32) for f in (stress, velocity, adj_stress, adj_velocity, buoyancy)]
        + [pltpu.SemaphoreType.DMA((Y_GROUPS, 5))],
        "pack_y",
        pltpu.HBM,
        PACK_LIMIT,
    )(
        stress, velocity, adj_stress, adj_velocity, buoyancy
    )
    ya, yb = swap(msg_a, msg_b, "gy")

    speed = shape((3, 16, 16, 128))
    tensor = shape((6, 16, 16, 128))
    msg = shape((17, MSG_ROWS, 128))
    m_scratch = pltpu.VMEM((3, 20, 16, 128), F32)
    xa, xb, part_v, adj_part_v, edge, adj_edge = call(
        pack_x_kernel,
        (msg, msg, speed, speed, shape((10, 20, 16, 128)), shape((9, 20, 16, 128))),
        8,
        [m_scratch, m_scratch],
        "pack_x",
    )(stress, velocity, adj_stress, adj_velocity, buoyancy, ya, yb, angle)
    xa, xb = swap(xa, xb, "gx")
    frame_v, adj_frame_v = pl.pallas_call(
        frame_kernel,
        out_shape=(speed, speed),
        in_specs=[whole()] * 4,
        out_specs=(whole(), whole()),
        compiler_params=pltpu.CompilerParams(vmem_limit_bytes=VMEM_LIMIT),
        name="frame",
    )(stress, adj_stress, edge, adj_edge)

    v_scratch = [pltpu.VMEM((3, 20, 16, 128), F32)] + [pltpu.VMEM((3, 16, 16, 128), F32)] * 2
    buoyancy_edge = edge[9:10]
    tile = shape((16, 128))
    velocity_next, stress_next, part, part_a, part_b, trig = call(
        forward_kernel,
        (speed, tensor, tile, tile, tile, shape((3,) + slots)),
        13,
        v_scratch
        + [
            pltpu.VMEM((3, 16, 16, 128), F32),
            pltpu.VMEM(slots, jnp.int32),
            pltpu.VMEM((768, 256), BF16),
            pltpu.VMEM((4,) + slots, F32),
            pltpu.VMEM((3,) + slots, F32),
        ],
        "forward",
    )(
        stress, part_v, frame_v, buoyancy, buoyancy_edge, lame_lambda, shear_modulus, xa, xb,
        cell, chan, weight, angle,
    )

    part_a, part_b = swap(part_a, part_b, "gx")
    adj_velocity_next, pulled = call(
        functools.partial(step_kernel, -1.0, 8), (speed, tensor), 9, v_scratch, "step_adj"
    )(adj_stress, adj_part_v, adj_frame_v, buoyancy, buoyancy_edge, lame_lambda, shear_modulus, xa, xb)

    predicted = part + part_a + part_b
    misfit = predicted - observed.reshape(16, 128)
    robust = misfit / jnp.sqrt(HUBER_SQUARE + misfit * misfit)
    robust_a, robust_b = swap(robust, robust, "gx")

    adj_stress_next = call(
        deposit_kernel,
        shape((6, 256, 128)),
        7,
        [
            pltpu.VMEM(slots, jnp.int32),
            pltpu.VMEM((7,) + slots, F32),
            pltpu.VMEM((768, 256), F32),
        ],
        "deposit",
    )(cell, chan, trig, robust_a, robust, robust_b, pulled.reshape(6, 256, 128)).reshape(tensor.shape)
    return (velocity_next, stress_next, predicted.reshape(1, owned), adj_velocity_next, adj_stress_next)


def solution(mesh):
    field = P(None, None, "gx", "gy")
    scalar = P(None, "gx", "gy")
    slot = P("gx", "gy", None)
    row = P("gy", "gx")
    return jax.shard_map(
        shards,
        mesh=mesh,
        in_specs=(field,) * 4 + (scalar,) * 3 + (slot,) * 3 + (row,) * 2,
        out_specs=(field, field, row, field, field),
        check_vma=False,
    )
```
